256 devices in a mesh: seq: 32 (over z, x_hi, core), head: 8 (over x_lo, y).
Axes of the slice: x: 4 (x_hi: 2, x_lo: 2; x = x_hi * 2 + x_lo), y: 4, z: 8, core: 2. Of those that a mesh axis runs over, the one named last changes fastest.
Arguments:
- q_nope: bfloat16 [4096, 8192], P('seq', 'head'), may hold values from -6 to 6
- q_rope: bfloat16 [4096, 4096], P('seq', 'head'), may hold values from -16 to 16
- kv_latent: bfloat16 [4096, 576], P('seq'), may hold values from -500 to 500
- positions: int32 [4096], P('seq'), may hold values from 0 to 4095, as said below
- kv_gain: float32 [512], replicated, may hold values from 0.5 to 2
- kv_up: bfloat16 [512, 16384], P(None, 'head'), may hold values from -0.25 to 0.25
- w_out: bfloat16 [8192, 7168], P('head', 'seq'), may hold values from -0.125 to 0.125
Outputs:
- mixed: bfloat16 [4096, 7168], P('seq', 'head')
The draws below stay inside these ranges and needn't reach their ends.
Inputs may be any that keep to these rules, and one draw needn't show every extreme that they name: The positions of each aligned block of 128 rows are consecutive and ascending and start at a multiple of 128; all positions together hold every number from 0 to 4095 once.
All inputs are finite; a program needn't handle non-finite values.
Results may differ from the reference program's by a relative error of at most 0.02.
Values may be sent and summed in bfloat16 or wider, within the bound.
A program may use at most 64 MiB of HBM per device.

```python
import math
import jax
import jax.numpy as jnp
from jax import lax

D = 7168
KV_RANK = 512
ROPE = 64
NOPE = 128
VDIM = 128
TOK_DEV = 128
HEADS = 64
TOKENS = 4096


def rope_normals(key):
    return jnp.clip(jax.random.normal(key, (TOKENS, ROPE), jnp.float32), -5.0, 5.0)


def draw_kv_latent(key, part):
    base = rope_normals(key)
    key = jax.random.fold_in(key, 11)
    first, second, third = jax.random.split(key, 3)
    row_scale = jnp.exp(jax.random.uniform(second, (TOKENS, 1), jnp.float32, 0.0, math.log(10.0)))
    col_scale = jnp.exp(jax.random.uniform(third, (1, KV_RANK), jnp.float32, 0.0, math.log(10.0)))
    coded = jnp.clip(jax.random.normal(first, (TOKENS, KV_RANK), jnp.float32), -5.0, 5.0)
    rope = base
    latent = coded * row_scale * col_scale
    return jnp.concatenate([latent, rope], axis=1).astype(jnp.bfloat16)


def draw_q_rope(key, part):
    key = jax.random.fold_in(key, 23)
    drawn = jnp.clip(jax.random.normal(key, (TOKENS, HEADS * ROPE), jnp.float32), -5.0, 5.0)
    return drawn.astype(jnp.bfloat16)


def draw_positions(key, part):
    key = jax.random.fold_in(key, 37)
    blocks = TOKENS // TOK_DEV
    order = jax.random.permutation(key, blocks).astype(jnp.int32)
    placed = order[:, None] * TOK_DEV + jnp.arange(TOK_DEV, dtype=jnp.int32)[None, :]
    return placed.reshape(TOKENS).astype(jnp.int32)


def with_spikes(values, key, source, target, blocks, factor):
    owner, partner = [(jnp.arange(values.shape[axis_at]) // (values.shape[axis_at] // blocks)).reshape([-1 if axis == axis_at else 1 for axis in range(values.ndim)]) for axis_at in (source, target)]
    chosen = jax.random.permutation(key, blocks)[partner]
    strong = (owner == chosen) | (owner == (partner + blocks // 2) % blocks)
    return jnp.where(strong, factor * values, values)


def block_levels(own_key, extent, pieces, least, largest):
    def one(dim, shards_of):
        steps = jax.random.uniform(jax.random.fold_in(jax.random.fold_in(own_key, 6), dim), (shards_of,), jnp.float32, least / len(pieces), largest / len(pieces))
        return jnp.repeat(jnp.exp(steps), extent[dim] // shards_of).reshape((-1,) + (1,) * (len(extent) - dim - 1))

    loudness = one(*pieces[0])
    for cut in pieces[1:]:
        loudness = loudness * one(*cut)
    return loudness


def centred(stream_key, dims, width, most, pieces=(), kind=jnp.bfloat16):
    entries = jax.random.normal(stream_key, dims, jnp.float32) * width
    if len(pieces) > 0:
        entries = block_levels(stream_key, dims, pieces, -0.22, 0.18) * entries
    return jnp.clip(entries, min=-most, max=most).astype(kind)


def gaussian_with(own_key, shape, spread, bound, cuts, heavy, held_as=jnp.bfloat16):
    result = spread * jax.random.normal(own_key, shape, jnp.float32)
    if cuts:
        result = result * block_levels(own_key, shape, cuts, -0.22, 0.18)
    return jnp.clip(with_spikes(result, jax.random.fold_in(own_key, 3), *heavy), -bound, bound).astype(held_as)


def setup_inputs(seed: int = 0) -> dict:
    key_list = jax.random.split(jax.random.key(seed), 8)
    return {
        "q_nope": centred(key_list[0], (TOKENS, HEADS * NOPE), 1.0, 6.0, ((0, 32), (1, 8))),
        "q_rope": draw_q_rope(jax.random.fold_in(key_list[7], 71), 0),
        "kv_latent": draw_kv_latent(jax.random.fold_in(key_list[7], 71), 0),
        "positions": draw_positions(jax.random.fold_in(key_list[7], 71), 0),
        "kv_gain": jnp.clip(jnp.exp(jax.random.uniform(key_list[4], (KV_RANK,), jnp.float32, math.log(0.5), math.log(2.0))), 0.5, 2.0),
        "kv_up": centred(key_list[5], (KV_RANK, HEADS * (NOPE + VDIM)), KV_RANK ** -0.5, 0.25, ((1, 8),)),
        "w_out": gaussian_with(key_list[6], (HEADS * VDIM, D), (HEADS * VDIM) ** -0.5, 0.125, ((0, 8), (1, 32)), (0, 1, 32, 2.75)),
    }


def reference(q_nope, q_rope, kv_latent, positions, kv_gain, kv_up, w_out):
    heads = q_nope.shape[1] // NOPE
    scale = 1.0 / math.sqrt(NOPE + ROPE)
    coded = kv_latent[:, :KV_RANK].astype(jnp.float32)
    latent = (coded * lax.rsqrt(lax.optimization_barrier(jnp.mean(coded * coded, axis=1, keepdims=True)) + 1e-06) * kv_gain).astype(jnp.bfloat16)
    key_rope = kv_latent[:, KV_RANK:]
    keys_values = jnp.dot(latent, kv_up, preferred_element_type=jnp.float32).astype(jnp.bfloat16)
    keys_values = keys_values.reshape(TOKENS, heads, NOPE + VDIM).transpose(1, 0, 2)
    key_nope = keys_values[:, :, :NOPE]
    values = keys_values[:, :, NOPE:]
    query_nope = q_nope.reshape(TOKENS, heads, NOPE).transpose(1, 0, 2)
    query_rope = q_rope.reshape(TOKENS, heads, ROPE).transpose(1, 0, 2)
    visible = positions[:, None] >= positions[None, :]

    def one_head(operands):
        qn, qr, kn, vv = operands
        scores = jnp.dot(qn, kn.T, preferred_element_type=jnp.float32) + jnp.dot(qr, key_rope.T, preferred_element_type=jnp.float32)
        scores = jnp.where(visible, scores * scale, -jnp.inf)
        expo = jnp.exp(scores - lax.optimization_barrier(jnp.max(scores, axis=1, keepdims=True)))
        total = lax.optimization_barrier(jnp.sum(expo, axis=1, keepdims=True))
        probs = expo.astype(jnp.bfloat16)
        return (jnp.dot(probs, vv, preferred_element_type=jnp.float32) / total).astype(jnp.bfloat16)
    attended = lax.map(one_head, (query_nope, query_rope, key_nope, values))
    attended = attended.transpose(1, 0, 2).reshape(TOKENS, heads * VDIM)
    return jnp.dot(attended, w_out, preferred_element_type=jnp.float32).astype(jnp.bfloat16)
```

```python
import functools
import math

import jax
import jax.numpy as jnp
from jax import lax
from jax.experimental import pallas as pl
from jax.experimental.pallas import tpu as pltpu
from jax.sharding import PartitionSpec as P

KV_RANK = 512
ROPE = 64
NOPE = 128
VDIM = 128
ROWS = 128
HEADS = 8
WIDE = 640
HIDDEN = -1e30
MESH = pl.DeviceIdType.MESH
F32 = jnp.float32
BF16 = jnp.bfloat16


def place():
    s, h = lax.axis_index("seq"), lax.axis_index("head")
    return s // 4, lax.rem(s // 2, 2), lax.rem(s, 2), h // 4, lax.rem(h, 4)


def at(z, xh, c, xl, y):
    return (lax.rem(z + 8, 8) * 4 + xh * 2 + c, xl * 4 + lax.rem(y + 4, 4))


def dot_nt(a, b):
    return lax.dot_general(a, b, (((1,), (1,)), ((), ())), preferred_element_type=F32)


def attention_kernel(
    pos_ref, lat_ref, gain_ref, qn_hbm, qr_hbm, up_hbm, att_ref,
    keys, qn, qr, up, query, top, total, summed,
    local_sem, x_send, x_recv, c_send, c_recv, z_send, z_recv, y_send, y_recv, d_send, d_recv,
):
    z, xh, c, xl, y = place()
    loads = [
        pltpu.make_async_copy(qn_hbm, qn, local_sem.at[0]),
        pltpu.make_async_copy(up_hbm, up, local_sem.at[1]),
        pltpu.make_async_copy(qr_hbm, qr, local_sem.at[2]),
    ]
    for load in loads:
        load.start()
    across = at(z, 1 - xh, c, 1 - xl, y)
    partner = at(z, xh, 1 - c, xl, y)
    right, left = at(z + 1, xh, c, xl, y), at(z - 1, xh, c, xl, y)
    above, below = at(z, xh, c, xl, y + 1), at(z, xh, c, xl, y - 1)
    barrier = pltpu.get_barrier_semaphore()
    for peer in (across, partner, right, left, above, below):
        pl.semaphore_signal(barrier, inc=1, device_id=peer, device_id_type=MESH)

    block_no = pos_ref[0] // ROWS
    lane = lax.broadcasted_iota(jnp.int32, (ROWS, 128), 1)
    coded = lat_ref[:, :KV_RANK].astype(F32)
    latent = coded * lax.rsqrt(jnp.mean(coded * coded, axis=1, keepdims=True) + 1e-06) * gain_ref[...]
    keys[z, xh, c, :, :KV_RANK] = latent.astype(BF16)
    rope = lat_ref[:, KV_RANK:].astype(F32)
    tail = jnp.concatenate([rope, jnp.zeros((ROWS, 64), F32)], axis=1)
    keys[z, xh, c, :, KV_RANK:] = jnp.where(lane == 64 + block_no, 1.0, tail).astype(BF16)
    pl.semaphore_wait(barrier, 6)

    half = pl.multiple_of(lax.rem(y, 2) * 64, 64)
    other = pl.multiple_of(64 - half, 64)
    half_hi = pl.multiple_of(half + 32, 32)
    other_hi = pl.multiple_of(other + 32, 32)

    def remote(ref, send, recv, peer):
        return pltpu.make_async_remote_copy(
            src_ref=ref, dst_ref=ref, send_sem=send, recv_sem=recv, device_id=peer, device_id_type=MESH
        )

    sent = []

    def push(ref, send, recv, peer):
        copy = remote(ref, send, recv, peer)
        copy.start()
        sent.append(copy)

    def landed(ref, send, recv):
        remote(ref, send, recv, partner).wait_recv()

    slab = lambda k: lax.rem(z + k + 8, 8)
    slots = {-1: 0, 1: 1, -2: 2, 2: 3, -3: 4, 3: 5, 4: 6}

    push(keys.at[z, xh, c, pl.ds(half, 64)], x_send.at[0], x_recv.at[0], across)
    push(keys.at[z, xh, c, pl.ds(other, 64)], x_send.at[1], x_recv.at[1], across)
    push(keys.at[z, xh, c], c_send.at[0], c_recv.at[0], partner)

    def prepare():
        loads[0].wait()
        loads[1].wait()
        loads[2].wait()
        ahead = jnp.where((lane >= 64) & (lane - 64 > block_no) & (lane < 96), HIDDEN, 0.0)
        for h in range(HEADS):
            rows = pl.ds(h * ROWS, ROWS)
            folded = dot_nt(qn[:, h * NOPE : (h + 1) * NOPE], up[:, h * 256 : h * 256 + NOPE])
            query[rows, :KV_RANK] = folded.astype(BF16)
            turned = qr[:, h * ROPE : (h + 1) * ROPE].astype(F32)
            turned = jnp.concatenate([turned, jnp.zeros((ROWS, 64), F32)], axis=1)
            query[rows, KV_RANK:] = (turned + ahead).astype(BF16)

    factor = math.log2(math.e) / math.sqrt(NOPE + ROPE)

    def attend(offsets, part, first=False):
        rows = pl.ds(part * 256, 256)
        q = query[rows, :]
        blocks = [keys[slab(k)].reshape(512, WIDE) for k in offsets]
        scores = [dot_nt(q, block) for block in blocks]
        if first:
            own = xh * 256 + c * ROWS
            token = lax.rem(lax.broadcasted_iota(jnp.int32, (256, 512), 0), ROWS)
            ahead = lax.broadcasted_iota(jnp.int32, (256, 512), 1) - own
            scores[0] = jnp.where((ahead > token) & (ahead < ROWS), HIDDEN, scores[0])
        most = functools.reduce(jnp.maximum, [jnp.max(s, axis=1, keepdims=True) for s in scores])
        if not first:
            before = top[rows, :1]
            most = jnp.maximum(most, before)
            fade = jnp.exp2((before - most) * factor)
        adds, totals = [], []
        for s, block in zip(scores, blocks):
            expo = jnp.exp2((s - most) * factor)
            for i in range(4):
                totals.append(expo[:, i * 128 : (i + 1) * 128])
            adds.append(jnp.dot(expo.astype(BF16), block[:, :KV_RANK], preferred_element_type=F32))
        gain = functools.reduce(jnp.add, adds)
        mass = functools.reduce(jnp.add, totals)
        if first:
            summed[rows, :] = gain
            total[rows, :] = mass
        else:
            summed[rows, :] = summed[rows, :] * fade + gain
            total[rows, :] = total[rows, :] * fade + mass
        top[rows, :] = jnp.broadcast_to(most, (256, 128))

    def from_z(d):
        for k, way, forward in ((-d, 0, right), (d, 1, left)):
            if d < 4:
                ref = keys.at[slab(k), :, c, pl.ds(half, 64)]
                landed(ref, z_send.at[way, d - 1], z_recv.at[way, d - 1])
                if d < 3:
                    push(ref, z_send.at[way, d], z_recv.at[way, d], forward)
                else:
                    push(keys.at[slab(k), way, c, pl.ds(half, 64)], z_send.at[way, 3], z_recv.at[way, 3], forward)
            else:
                landed(keys.at[slab(4), way, c, pl.ds(half, 64)], z_send.at[way, 3], z_recv.at[way, 3])
        for k in (-d, d) if d < 4 else (4,):
            i = slots[k]
            push(keys.at[slab(k), :, c, pl.ds(half, 32)], y_send.at[0, i], y_recv.at[0, i], above)
            push(keys.at[slab(k), :, c, pl.ds(half_hi, 32)], y_send.at[1, i], y_recv.at[1, i], below)
            push(keys.at[slab(k), :, c, pl.ds(half, 64)], d_send.at[0, i], d_recv.at[0, i], partner)

    def from_y(d):
        for k in (-d, d) if d < 4 else (4,):
            i = slots[k]
            landed(keys.at[slab(k), :, c, pl.ds(other, 32)], y_send.at[0, i], y_recv.at[0, i])
            landed(keys.at[slab(k), :, c, pl.ds(other_hi, 32)], y_send.at[1, i], y_recv.at[1, i])
            push(keys.at[slab(k), :, c, pl.ds(other, 64)], d_send.at[1, i], d_recv.at[1, i], partner)

    def ready(d):
        for k in (-d, d) if d < 4 else (4,):
            i = slots[k]
            landed(keys.at[slab(k), :, 1 - c, pl.ds(half, 64)], d_send.at[0, i], d_recv.at[0, i])
            landed(keys.at[slab(k), :, 1 - c, pl.ds(other, 64)], d_send.at[1, i], d_recv.at[1, i])

    prepare()
    landed(keys.at[z, 1 - xh, c, pl.ds(half, 64)], x_send.at[0], x_recv.at[0])
    start = keys.at[z, :, c, pl.ds(half, 64)]
    push(start, z_send.at[0, 0], z_recv.at[0, 0], right)
    push(start, z_send.at[1, 0], z_recv.at[1, 0], left)
    landed(keys.at[z, 1 - xh, c, pl.ds(other, 64)], x_send.at[1], x_recv.at[1])
    push(keys.at[z, 1 - xh, c], c_send.at[1], c_recv.at[1], partner)
    landed(keys.at[z, xh, 1 - c], c_send.at[0], c_recv.at[0])
    landed(keys.at[z, 1 - xh, 1 - c], c_send.at[1], c_recv.at[1])
    for part in range(4):
        attend((0,), part, first=True)
    from_z(1)
    from_y(1)
    ready(1)
    from_z(2)
    for part in range(4):
        attend((-1, 1), part)
        if part == 1:
            from_y(2)
        if part == 2:
            from_z(3)
    ready(2)
    for part in range(4):
        attend((-2, 2), part)
        if part == 0:
            from_y(3)
        if part == 1:
            from_z(4)
    ready(3)
    for part in range(4):
        attend((-3, 3), part)
        if part == 1:
            from_y(4)
    ready(4)
    for part in range(4):
        attend((4,), part)
    for h in range(HEADS):
        rows = pl.ds(h * ROWS, ROWS)
        share = summed[rows, :] / jnp.sum(total[rows, :], axis=1, keepdims=True)
        value = jnp.dot(share.astype(BF16), up[:, h * 256 + NOPE : (h + 1) * 256], preferred_element_type=F32)
        att_ref[:, h * VDIM : (h + 1) * VDIM] = value.astype(BF16)
    for copy in sent:
        copy.wait_send()


def attention(positions, kv_latent, gain, q_nope, q_rope, kv_up):
    dma = pltpu.SemaphoreType.DMA
    vmem, smem, any_ = (pl.BlockSpec(memory_space=m) for m in (pltpu.VMEM, pltpu.SMEM, pl.ANY))
    return pl.pallas_call(
        attention_kernel,
        out_shape=jax.ShapeDtypeStruct((ROWS, HEADS * VDIM), BF16),
        in_specs=[smem, vmem, vmem, any_, any_, any_],
        out_specs=vmem,
        scratch_shapes=[
            pltpu.VMEM((8, 2, 2, ROWS, WIDE), BF16),
            pltpu.VMEM((ROWS, HEADS * NOPE), BF16),
            pltpu.VMEM((ROWS, HEADS * ROPE), BF16),
            pltpu.VMEM((KV_RANK, HEADS * 256), BF16),
            pltpu.VMEM((HEADS * ROWS, WIDE), BF16),
            pltpu.VMEM((HEADS * ROWS, 128), F32),
            pltpu.VMEM((HEADS * ROWS, 128), F32),
            pltpu.VMEM((HEADS * ROWS, KV_RANK), F32),
            dma((3,)), dma((2,)), dma((2,)), dma((2,)), dma((2,)),
            dma((2, 4)), dma((2, 4)), dma((2, 7)), dma((2, 7)), dma((2, 7)), dma((2, 7)),
        ],
        compiler_params=pltpu.CompilerParams(
            collective_id=0, has_side_effects=True, vmem_limit_bytes=48 * 2**20
        ),
        cost_estimate=pl.CostEstimate(flops=11 * 10**9, bytes_accessed=4 * 10**6, transcendentals=4 * 10**6),
        name="attention",
    )(positions, kv_latent, gain, q_nope, q_rope, kv_up)


def project_kernel(
    att_ref, w_hbm, out_ref, held, w, part, reached, half_sum, final,
    w_sem, a_send, a_recv, y_send, y_recv, f_send, f_recv,
):
    z, xh, c, xl, y = place()
    head = xl * 4 + y
    load = pltpu.make_async_copy(w_hbm, w, w_sem)
    load.start()
    right, left = at(z + 1, xh, c, xl, y), at(z - 1, xh, c, xl, y)
    barrier = pltpu.get_barrier_semaphore()

    def greet(peer):
        pl.semaphore_signal(barrier, inc=1, device_id=peer, device_id_type=MESH)

    greet(right)
    greet(left)
    for j in (1, 2, 3):
        greet(at(z, xh, c, xl, y + j))
    for j in (0, 1):
        pl.when((head != z) | (xl != j))(lambda: greet(at(head, xh, c, j, lax.rem(z, 4))))
    pl.semaphore_wait(barrier, jnp.where(head == z, 6, 7))

    def remote(src, dst, send, recv, peer):
        return pltpu.make_async_remote_copy(
            src_ref=src, dst_ref=dst, send_sem=send, recv_sem=recv, device_id=peer, device_id_type=MESH
        )

    sent = []

    def push(src, dst, send, recv, peer):
        copy = remote(src, dst, send, recv, peer)
        copy.start()
        sent.append(copy)

    slab = lambda k: lax.rem(z + k + 8, 8)
    push(att_ref, held.at[z], a_send.at[0, 0], a_recv.at[0, 0], right)
    push(att_ref, held.at[z], a_send.at[1, 0], a_recv.at[1, 0], left)
    load.wait()
    order = (0, -1, 1, -2, 2, -3, 3, 4)

    def spread(i):
        block = slab(order[i])
        peer = at(z, xh, c, xl, lax.rem(block, 4))
        return remote(part.at[block], reached.at[block // 4, y], y_send.at[i], y_recv.at[block // 4, y], peer)

    def multiply(i):
        block = slab(order[i])
        a = att_ref[...] if i == 0 else held[block]
        part[block] = jnp.dot(a, w[...], preferred_element_type=F32).astype(BF16)
        pl.when(lax.rem(block, 4) != y)(lambda: spread(i).start())

    def collect(i):
        block = slab(order[i])
        k = block // 4

        @pl.when(lax.rem(block, 4) == y)
        def _():
            acc = part[block].astype(F32)
            for j in (1, 2, 3):
                who = lax.rem(y + j, 4)
                remote(part.at[block], reached.at[k, who], y_send.at[i], y_recv.at[k, who], right).wait_recv()
                acc = acc + reached[k, who].astype(F32)
            half_sum[k] = acc.astype(BF16)

            @pl.when((block == z) & (head == z))
            def _():
                pltpu.make_async_copy(half_sum.at[k], final.at[xl], f_recv.at[xl]).start()

            @pl.when((block != z) | (head != z))
            def _():
                peer = at(block, xh, c, z // 4, lax.rem(z, 4))
                remote(half_sum.at[k], final.at[xl], f_send.at[k], f_recv.at[xl], peer).start()

    multiply(0)
    for d in (1, 2, 3):
        for k, way, forward in ((-d, 0, right), (d, 1, left)):
            ref = held.at[slab(k)]
            remote(ref, ref, a_send.at[way, d - 1], a_recv.at[way, d - 1], right).wait_recv()
            if d < 3:
                push(ref, ref, a_send.at[way, d], a_recv.at[way, d], forward)
            else:
                piece = held.at[slab(k), pl.ds(way * 64, 64)]
                push(piece, piece, a_send.at[way, 3], a_recv.at[way, 3], forward)
        multiply(2 * d - 1)
        multiply(2 * d)
        if d == 1:
            collect(0)
        else:
            collect(2 * d - 3)
            collect(2 * d - 2)
    for way in (0, 1):
        piece = held.at[slab(4), pl.ds(way * 64, 64)]
        remote(piece, piece, a_send.at[way, 3], a_recv.at[way, 3], right).wait_recv()
    multiply(7)
    collect(5)
    collect(6)
    collect(7)
    for j in (0, 1):
        remote(half_sum.at[0], final.at[j], f_send.at[0], f_recv.at[j], right).wait_recv()
    out_ref[...] = (final[0].astype(F32) + final[1].astype(F32)).astype(BF16)
    for copy in sent:
        copy.wait_send()
    for i in range(8):
        pl.when(lax.rem(slab(order[i]), 4) != y)(lambda: spread(i).wait_send())
    for k in (0, 1):
        block = y + 4 * k

        @pl.when((block != z) | (head != z))
        def _():
            remote(half_sum.at[k], final.at[xl], f_send.at[k], f_recv.at[xl], right).wait_send()


def project(att, w):
    dma = pltpu.SemaphoreType.DMA
    vmem, any_ = (pl.BlockSpec(memory_space=m) for m in (pltpu.VMEM, pl.ANY))
    columns = w.shape[1]
    return pl.pallas_call(
        project_kernel,
        out_shape=jax.ShapeDtypeStruct((ROWS, columns), BF16),
        in_specs=[vmem, any_],
        out_specs=vmem,
        scratch_shapes=[
            pltpu.VMEM((8, ROWS, HEADS * VDIM), BF16),
            pltpu.VMEM((HEADS * VDIM, columns), BF16),
            pltpu.VMEM((8, ROWS, columns), BF16),
            pltpu.VMEM((2, 4, ROWS, columns), BF16),
            pltpu.VMEM((2, ROWS, columns), BF16),
            pltpu.VMEM((2, ROWS, columns), BF16),
            dma(()), dma((2, 4)), dma((2, 4)), dma((8,)), dma((2, 4)), dma((2,)), dma((2,)),
        ],
        compiler_params=pltpu.CompilerParams(
            collective_id=1, has_side_effects=True, vmem_limit_bytes=48 * 2**20
        ),
        cost_estimate=pl.CostEstimate(flops=2 * 10**9, bytes_accessed=4 * 10**6, transcendentals=0),
        name="project",
    )(att, w)


def local(q_nope, q_rope, kv_latent, positions, kv_gain, kv_up, w_out):
    groups = [[4 * z + i for i in range(4)] for z in range(8)]
    w = lax.all_gather(w_out, "seq", axis=1, tiled=True, axis_index_groups=groups)
    att = attention(positions, kv_latent, kv_gain.reshape(1, KV_RANK), q_nope, q_rope, kv_up)
    return project(att, w)


def solution(mesh):
    return jax.shard_map(
        local,
        mesh=mesh,
        in_specs=(
            P("seq", "head"),
            P("seq", "head"),
            P("seq", None),
            P("seq"),
            P(),
            P(None, "head"),
            P("head", "seq"),
        ),
        out_specs=P("seq", "head"),
        check_vma=False,
    )
```

```python
import functools
import math

import jax
import jax.numpy as jnp
from jax import lax
from jax.experimental import pallas as pl
from jax.experimental.pallas import tpu as pltpu
from jax.sharding import PartitionSpec as P

KV_RANK = 512
ROPE = 64
NOPE = 128
VDIM = 128
ROWS = 128
HEADS = 8
WIDE = 640
HIDDEN = -1e30
MESH = pl.DeviceIdType.MESH
F32 = jnp.float32
BF16 = jnp.bfloat16


def place():
    s, h = lax.axis_index("seq"), lax.axis_index("head")
    return s // 4, lax.rem(s // 2, 2), lax.rem(s, 2), h // 4, lax.rem(h, 4)


def at(z, xh, c, xl, y):
    return (lax.rem(z + 8, 8) * 4 + xh * 2 + c, xl * 4 + lax.rem(y + 4, 4))


def dot_nt(a, b):
    return lax.dot_general(a, b, (((1,), (1,)), ((), ())), preferred_element_type=F32)


def attention_kernel(
    pos_hbm, lat_hbm, gain_hbm, qn_hbm, qr_hbm, up_hbm, att_ref,
    pos_ref, lat_ref, gain_ref, keys, qn, qr, up, query, top, total, summed,
    local_sem, x_send, x_recv, c_send, c_recv, z_send, z_recv, y_send, y_recv, d_send, d_recv,
):
    z, xh, c, xl, y = place()
    first_loads = [
        pltpu.make_async_copy(lat_hbm, lat_ref, local_sem.at[3]),
        pltpu.make_async_copy(gain_hbm, gain_ref, local_sem.at[4]),
        pltpu.make_async_copy(pos_hbm, pos_ref, local_sem.at[5]),
    ]
    for load in first_loads:
        load.start()
    loads = [
        pltpu.make_async_copy(qn_hbm, qn, local_sem.at[0]),
        pltpu.make_async_copy(up_hbm, up, local_sem.at[1]),
        pltpu.make_async_copy(qr_hbm, qr, local_sem.at[2]),
    ]
    for load in loads:
        load.start()
    across = at(z, 1 - xh, c, 1 - xl, y)
    partner = at(z, xh, 1 - c, xl, y)
    right, left = at(z + 1, xh, c, xl, y), at(z - 1, xh, c, xl, y)
    above, below = at(z, xh, c, xl, y + 1), at(z, xh, c, xl, y - 1)
    barrier = pltpu.get_barrier_semaphore()
    for peer in (across, partner, right, left, above, below):
        pl.semaphore_signal(barrier, inc=1, device_id=peer, device_id_type=MESH)

    for load in first_loads:
        load.wait()
    block_no = pos_ref[0] // ROWS
    lane = lax.broadcasted_iota(jnp.int32, (ROWS, 128), 1)
    coded = lat_ref[:KV_RANK, :].astype(F32).T
    latent = coded * lax.rsqrt(jnp.mean(coded * coded, axis=1, keepdims=True) + 1e-06) * gain_ref[...].reshape(1, KV_RANK)
    keys[z, xh, c, :, :KV_RANK] = latent.astype(BF16)
    rope = lat_ref[KV_RANK:, :].astype(F32)
    tail = jnp.concatenate([rope, jnp.zeros((64, ROWS), F32)], axis=0).T
    keys[z, xh, c, :, KV_RANK:] = jnp.where(lane == 64 + block_no, 1.0, tail).astype(BF16)
    pl.semaphore_wait(barrier, 6)

    half = pl.multiple_of(lax.rem(y, 2) * 64, 64)
    other = pl.multiple_of(64 - half, 64)
    half_hi = pl.multiple_of(half + 32, 32)
    other_hi = pl.multiple_of(other + 32, 32)

    def remote(ref, send, recv, peer):
        return pltpu.make_async_remote_copy(
            src_ref=ref, dst_ref=ref, send_sem=send, recv_sem=recv, device_id=peer, device_id_type=MESH
        )

    sent = []

    def push(ref, send, recv, peer):
        copy = remote(ref, send, recv, peer)
        copy.start()
        sent.append(copy)

    def landed(ref, send, recv):
        remote(ref, send, recv, partner).wait_recv()

    slab = lambda k: lax.rem(z + k + 8, 8)
    slots = {-1: 0, 1: 1, -2: 2, 2: 3, -3: 4, 3: 5, 4: 6}

    push(keys.at[z, xh, c, pl.ds(half, 64)], x_send.at[0], x_recv.at[0], across)
    push(keys.at[z, xh, c, pl.ds(other, 64)], x_send.at[1], x_recv.at[1], across)
    push(keys.at[z, xh, c], c_send.at[0], c_recv.at[0], partner)

    def prepare():
        loads[0].wait()
        loads[1].wait()
        loads[2].wait()
        ahead = jnp.where((lane >= 64) & (lane - 64 > block_no) & (lane < 96), HIDDEN, 0.0)
        for h in range(HEADS):
            rows = pl.ds(h * ROWS, ROWS)
            folded = dot_nt(qn[:, h * NOPE : (h + 1) * NOPE], up[:, h * 256 : h * 256 + NOPE])
            query[rows, :KV_RANK] = folded.astype(BF16)
            turned = qr[:, h * ROPE : (h + 1) * ROPE].astype(F32)
            turned = jnp.concatenate([turned, jnp.zeros((ROWS, 64), F32)], axis=1)
            query[rows, KV_RANK:] = (turned + ahead).astype(BF16)

    factor = math.log2(math.e) / math.sqrt(NOPE + ROPE)

    def attend(offsets, part, first=False):
        rows = pl.ds(part * 256, 256)
        q = query[rows, :]
        blocks = [keys[slab(k)].reshape(512, WIDE) for k in offsets]
        scores = [dot_nt(q, block) for block in blocks]
        if first:
            own = xh * 256 + c * ROWS
            token = lax.rem(lax.broadcasted_iota(jnp.int32, (256, 512), 0), ROWS)
            ahead = lax.broadcasted_iota(jnp.int32, (256, 512), 1) - own
            scores[0] = jnp.where((ahead > token) & (ahead < ROWS), HIDDEN, scores[0])
        most = functools.reduce(jnp.maximum, [jnp.max(s, axis=1, keepdims=True) for s in scores])
        if not first:
            before = top[rows, :1]
            most = jnp.maximum(most, before)
            fade = jnp.exp2((before - most) * factor)
        adds, totals = [], []
        for s, block in zip(scores, blocks):
            expo = jnp.exp2((s - most) * factor)
            for i in range(4):
                totals.append(expo[:, i * 128 : (i + 1) * 128])
            adds.append(jnp.dot(expo.astype(BF16), block[:, :KV_RANK], preferred_element_type=F32))
        gain = functools.reduce(jnp.add, adds)
        mass = functools.reduce(jnp.add, totals)
        if first:
            summed[rows, :] = gain
            total[rows, :] = mass
        else:
            summed[rows, :] = summed[rows, :] * fade + gain
            total[rows, :] = total[rows, :] * fade + mass
        top[rows, :] = jnp.broadcast_to(most, (256, 128))

    def from_z(d):
        for k, way, forward in ((-d, 0, right), (d, 1, left)):
            if d < 4:
                ref = keys.at[slab(k), :, c, pl.ds(half, 64)]
                landed(ref, z_send.at[way, d - 1], z_recv.at[way, d - 1])
                if d < 3:
                    push(ref, z_send.at[way, d], z_recv.at[way, d], forward)
                else:
                    push(keys.at[slab(k), way, c, pl.ds(half, 64)], z_send.at[way, 3], z_recv.at[way, 3], forward)
            else:
                landed(keys.at[slab(4), way, c, pl.ds(half, 64)], z_send.at[way, 3], z_recv.at[way, 3])
        for k in (-d, d) if d < 4 else (4,):
            i = slots[k]
            push(keys.at[slab(k), :, c, pl.ds(half, 32)], y_send.at[0, i], y_recv.at[0, i], above)
            push(keys.at[slab(k), :, c, pl.ds(half_hi, 32)], y_send.at[1, i], y_recv.at[1, i], below)
            push(keys.at[slab(k), :, c, pl.ds(half, 64)], d_send.at[0, i], d_recv.at[0, i], partner)

    def from_y(d):
        for k in (-d, d) if d < 4 else (4,):
            i = slots[k]
            landed(keys.at[slab(k), :, c, pl.ds(other, 32)], y_send.at[0, i], y_recv.at[0, i])
            landed(keys.at[slab(k), :, c, pl.ds(other_hi, 32)], y_send.at[1, i], y_recv.at[1, i])
            push(keys.at[slab(k), :, c, pl.ds(other, 64)], d_send.at[1, i], d_recv.at[1, i], partner)

    def ready(d):
        for k in (-d, d) if d < 4 else (4,):
            i = slots[k]
            landed(keys.at[slab(k), :, 1 - c, pl.ds(half, 64)], d_send.at[0, i], d_recv.at[0, i])
            landed(keys.at[slab(k), :, 1 - c, pl.ds(other, 64)], d_send.at[1, i], d_recv.at[1, i])

    prepare()
    landed(keys.at[z, 1 - xh, c, pl.ds(half, 64)], x_send.at[0], x_recv.at[0])
    start = keys.at[z, :, c, pl.ds(half, 64)]
    push(start, z_send.at[0, 0], z_recv.at[0, 0], right)
    push(start, z_send.at[1, 0], z_recv.at[1, 0], left)
    landed(keys.at[z, 1 - xh, c, pl.ds(other, 64)], x_send.at[1], x_recv.at[1])
    push(keys.at[z, 1 - xh, c], c_send.at[1], c_recv.at[1], partner)
    landed(keys.at[z, xh, 1 - c], c_send.at[0], c_recv.at[0])
    landed(keys.at[z, 1 - xh, 1 - c], c_send.at[1], c_recv.at[1])
    for part in range(4):
        attend((0,), part, first=True)
    from_z(1)
    from_y(1)
    ready(1)
    from_z(2)
    for part in range(4):
        attend((-1, 1), part)
        if part == 1:
            from_y(2)
        if part == 2:
            from_z(3)
    ready(2)
    for part in range(4):
        attend((-2, 2), part)
        if part == 0:
            from_y(3)
        if part == 1:
            from_z(4)
    ready(3)
    for part in range(4):
        attend((-3, 3), part)
        if part == 1:
            from_y(4)
    ready(4)
    for part in range(4):
        attend((4,), part)
    for h in range(HEADS):
        rows = pl.ds(h * ROWS, ROWS)
        share = summed[rows, :] / jnp.sum(total[rows, :], axis=1, keepdims=True)
        value = jnp.dot(share.astype(BF16), up[:, h * 256 + NOPE : (h + 1) * 256], preferred_element_type=F32)
        att_ref[:, h * VDIM : (h + 1) * VDIM] = value.astype(BF16)
    for copy in sent:
        copy.wait_send()


def attention(positions, kv_latent, gain, q_nope, q_rope, kv_up):
    dma = pltpu.SemaphoreType.DMA
    vmem, any_ = (pl.BlockSpec(memory_space=m) for m in (pltpu.VMEM, pl.ANY))
    return pl.pallas_call(
        attention_kernel,
        out_shape=jax.ShapeDtypeStruct((ROWS, HEADS * VDIM), BF16),
        in_specs=[any_] * 6,
        out_specs=vmem,
        scratch_shapes=[
            pltpu.SMEM((ROWS,), jnp.int32),
            pltpu.VMEM((KV_RANK + ROPE, ROWS), BF16),
            pltpu.VMEM((KV_RANK,), F32),
            pltpu.VMEM((8, 2, 2, ROWS, WIDE), BF16),
            pltpu.VMEM((ROWS, HEADS * NOPE), BF16),
            pltpu.VMEM((ROWS, HEADS * ROPE), BF16),
            pltpu.VMEM((KV_RANK, HEADS * 256), BF16),
            pltpu.VMEM((HEADS * ROWS, WIDE), BF16),
            pltpu.VMEM((HEADS * ROWS, 128), F32),
            pltpu.VMEM((HEADS * ROWS, 128), F32),
            pltpu.VMEM((HEADS * ROWS, KV_RANK), F32),
            dma((6,)), dma((2,)), dma((2,)), dma((2,)), dma((2,)),
            dma((2, 4)), dma((2, 4)), dma((2, 7)), dma((2, 7)), dma((2, 7)), dma((2, 7)),
        ],
        compiler_params=pltpu.CompilerParams(
            collective_id=0, has_side_effects=True, vmem_limit_bytes=60 * 2**20
        ),
        cost_estimate=pl.CostEstimate(flops=11 * 10**9, bytes_accessed=4 * 10**6, transcendentals=4 * 10**6),
        name="attention",
    )(positions, kv_latent, gain, q_nope, q_rope, kv_up)


def project_kernel(
    att_ref, w_hbm, out_ref, held, w, part, reached, done, final,
    w_sem, a_send, a_recv, s_send, s_recv, f_send, f_recv,
):
    z, xh, c, xl, y = place()
    head = xl * 4 + y
    load = pltpu.make_async_copy(w_hbm, w, w_sem)
    load.start()
    right, left = at(z + 1, xh, c, xl, y), at(z - 1, xh, c, xl, y)
    barrier = pltpu.get_barrier_semaphore()
    seat = lambda plane, col: (lax.rem(plane, 8) * 4 + xh * 2 + c, lax.rem(col, 8))

    def greet(peer):
        pl.semaphore_signal(barrier, inc=1, device_id=peer, device_id_type=MESH)

    greet(right)
    greet(left)
    for j in range(1, 8):
        greet(seat(z, head + j))
    for j in range(8):
        pl.when((head != z) | (head != j))(lambda: greet(seat(head, j)))
    pl.semaphore_wait(barrier, jnp.where(head == z, 16, 17))

    def remote(src, dst, send, recv, peer):
        return pltpu.make_async_remote_copy(
            src_ref=src, dst_ref=dst, send_sem=send, recv_sem=recv, device_id=peer, device_id_type=MESH
        )

    sent = []

    def push(src, dst, send, recv, peer):
        copy = remote(src, dst, send, recv, peer)
        copy.start()
        sent.append(copy)

    slab = lambda k: lax.rem(z + k + 8, 8)
    for p in (0, 1):
        piece = pl.ds(p * 64, 64)
        push(att_ref.at[piece], held.at[z, piece], a_send.at[0, 0, p], a_recv.at[0, 0, p], right)
        push(att_ref.at[piece], held.at[z, piece], a_send.at[1, 0, p], a_recv.at[1, 0, p], left)
    load.wait()
    own = pl.ds(pl.multiple_of(head * 16, 16), 16)

    def multiply(k):
        block = slab(k)
        a = att_ref[...] if k == 0 else held[block]
        part[block] = dot_nt(a, w[...]).astype(BF16)
        for j in range(1, 8):
            rows = pl.ds(pl.multiple_of(lax.rem(head + j, 8) * 16, 16), 16)
            remote(
                part.at[block, rows], reached.at[block, j - 1], s_send.at[block], s_recv.at[block], seat(z, head + j)
            ).start()

    def collect(k):
        block = slab(k)
        everything = reached.at[block]
        remote(everything, everything, s_send.at[block], s_recv.at[block], right).wait_recv()
        acc = part[block, own].astype(F32)
        for j in range(7):
            acc = acc + reached[block, j].astype(F32)
        done[block] = acc.astype(BF16)
        if k == 0:

            @pl.when(head == z)
            def _():
                pltpu.make_async_copy(done.at[block], final.at[own], f_recv).start()

            @pl.when(head != z)
            def _():
                remote(done.at[block], final.at[own], f_send.at[0], f_recv, seat(block, z)).start()
        else:
            push(done.at[block], final.at[own], f_send.at[k + 3], f_recv, seat(block, z))

    multiply(0)
    for d in (1, 2, 3):
        for p in (0, 1):
            for k, way, forward in ((-d, 0, right), (d, 1, left)):
                ref = held.at[slab(k), pl.ds(p * 64, 64)]
                remote(ref, ref, a_send.at[way, d - 1, p], a_recv.at[way, d - 1, p], right).wait_recv()
                if d < 3 or p == way:
                    push(ref, ref, a_send.at[way, d, p], a_recv.at[way, d, p], forward)
        multiply(-d)
        multiply(d)
        if d == 1:
            collect(0)
        else:
            collect(1 - d)
            collect(d - 1)
    for way in (0, 1):
        ref = held.at[slab(4), pl.ds(way * 64, 64)]
        remote(ref, ref, a_send.at[way, 3, way], a_recv.at[way, 3, way], right).wait_recv()
    multiply(4)
    collect(-3)
    collect(3)
    collect(4)
    remote(final, final, f_send.at[0], f_recv, right).wait_recv()
    out_ref[...] = final[...]
    for copy in sent:
        copy.wait_send()
    for block in range(8):
        everything = reached.at[block]
        remote(everything, everything, s_send.at[block], s_recv.at[block], right).wait_send()

    @pl.when(head != z)
    def _():
        remote(done.at[0], done.at[0], f_send.at[0], f_recv, right).wait_send()


def project(att, w):
    dma = pltpu.SemaphoreType.DMA
    vmem, any_ = (pl.BlockSpec(memory_space=m) for m in (pltpu.VMEM, pl.ANY))
    columns = w.shape[0]
    return pl.pallas_call(
        project_kernel,
        out_shape=jax.ShapeDtypeStruct((ROWS, columns), BF16),
        in_specs=[vmem, any_],
        out_specs=vmem,
        scratch_shapes=[
            pltpu.VMEM((8, ROWS, HEADS * VDIM), BF16),
            pltpu.VMEM(w.shape, BF16),
            pltpu.VMEM((8, ROWS, columns), BF16),
            pltpu.VMEM((8, 7, 16, columns), BF16),
            pltpu.VMEM((8, 16, columns), BF16),
            pltpu.VMEM((ROWS, columns), BF16),
            dma(()), dma((2, 4, 2)), dma((2, 4, 2)), dma((8,)), dma((8,)), dma((8,)), dma(()),
        ],
        compiler_params=pltpu.CompilerParams(
            collective_id=1, has_side_effects=True, vmem_limit_bytes=60 * 2**20
        ),
        cost_estimate=pl.CostEstimate(flops=2 * 10**9, bytes_accessed=4 * 10**6, transcendentals=0),
        name="project",
    )(att, w)


def local(q_nope, q_rope, kv_latent, positions, kv_gain, kv_up, w_out):
    groups = [[4 * z + i for i in range(4)] for z in range(8)]
    w = lax.all_gather(w_out.T, "seq", axis=0, tiled=True, axis_index_groups=groups)
    att = attention(positions, kv_latent.T, kv_gain, q_nope, q_rope, kv_up)
    return project(att, w)


def solution(mesh):
    return jax.shard_map(
        local,
        mesh=mesh,
        in_specs=(
            P("seq", "head"),
            P("seq", "head"),
            P("seq", None),
            P("seq"),
            P(),
            P(None, "head"),
            P("head", "seq"),
        ),
        out_specs=P("seq", "head"),
        check_vma=False,
    )
```

```python
import math

import jax
import jax.numpy as jnp
from jax import lax
from jax.experimental import pallas as pl
from jax.experimental.pallas import tpu as pltpu
from jax.sharding import PartitionSpec as P

KV_RANK = 512
ROPE = 64
NOPE = 128
VDIM = 128
ROWS = 128
HEADS = 8
WIDE = 640
PART = 256
HIDDEN = -1e30
MESH = pl.DeviceIdType.MESH
F32 = jnp.float32
BF16 = jnp.bfloat16


def dot_nt(a, b):
    return lax.dot_general(a, b, (((1,), (1,)), ((), ())), preferred_element_type=F32)


def kernel(
    pos_hbm, lat_hbm, gain_hbm, qn_hbm, qr_hbm, up_hbm, w_hbm, out_ref,
    pos_ref, lat_ref, gain_ref, keys, qn, qr, up, query, top, total, summed,
    held, w, part, reached, done, final,
    local_sem, x_send, x_recv, c_send, c_recv, z_send, z_recv, n_send, n_recv, d_send, d_recv,
    w_send, w_recv, a_send, a_recv, s_send, s_recv, f_send, f_recv,
):
    s, head = lax.axis_index("seq"), lax.axis_index("head")
    z, xh, c, xl, y = s // 4, lax.rem(s // 2, 2), lax.rem(s, 2), head // 4, lax.rem(head, 4)

    def at(z, xh, c, xl, y):
        return (lax.rem(z + 8, 8) * 4 + xh * 2 + c, xl * 4 + lax.rem(y + 4, 4))

    def seat(plane, col):
        return (lax.rem(plane, 8) * 4 + xh * 2 + c, lax.rem(col, 8))

    def slab(k):
        return lax.rem(z + k + 8, 8)

    across, beside = at(z, 1 - xh, c, 1 - xl, y), at(z, xh, c, 1 - xl, y)
    partner, opposite = at(z, xh, 1 - c, xl, y), at(z, 1 - xh, c, xl, y)
    right, left = at(z + 1, xh, c, xl, y), at(z - 1, xh, c, xl, y)
    above, below = at(z, xh, c, xl, y + 1), at(z, xh, c, xl, y - 1)

    def remote(src, dst, send, recv, peer):
        return pltpu.make_async_remote_copy(
            src_ref=src, dst_ref=dst, send_sem=send, recv_sem=recv, device_id=peer, device_id_type=MESH
        )

    sent = []

    def push(src, dst, send, recv, peer):
        copy = remote(src, dst, send, recv, peer)
        copy.start()
        sent.append(copy)

    def landed(ref, send, recv):
        remote(ref, ref, send, recv, partner).wait_recv()

    def load(src, dst, i):
        copy = pltpu.make_async_copy(src, dst, local_sem.at[i])
        copy.start()
        return copy

    w_own = w.at[pl.ds(pl.multiple_of((xh * 2 + c) * 224, 32), 224)]
    first_loads = [load(lat_hbm, lat_ref, 0), load(gain_hbm, gain_ref, 1), load(pos_hbm, pos_ref, 2)]
    loads = [load(qn_hbm, qn, 3), load(up_hbm, up, 4), load(qr_hbm, qr, 5)]

    barrier = pltpu.get_barrier_semaphore()

    def greet(peer):
        pl.semaphore_signal(barrier, inc=1, device_id=peer, device_id_type=MESH)

    for peer in (across, partner, opposite, right, left):
        greet(peer)
    for j in range(1, 8):
        greet(seat(z, head + j))
    for j in range(8):
        pl.when((head != z) | (head != j))(lambda: greet(seat(head, j)))

    for copy in first_loads:
        copy.wait()
    block_no = pos_ref[0] // ROWS
    lane = lax.broadcasted_iota(jnp.int32, (ROWS, 128), 1)
    coded = lat_ref[:KV_RANK, :].astype(F32).T
    latent = coded * lax.rsqrt(jnp.mean(coded * coded, axis=1, keepdims=True) + 1e-06)
    keys[z, xh, c, :, :KV_RANK] = (latent * gain_ref[...].reshape(1, KV_RANK)).astype(BF16)
    rope = lat_ref[KV_RANK:, :].astype(F32)
    tail = jnp.concatenate([rope, jnp.zeros((64, ROWS), F32)], axis=0).T
    keys[z, xh, c, :, KV_RANK:] = jnp.where(lane == 64 + block_no, 1.0, tail).astype(BF16)
    pl.semaphore_wait(barrier, jnp.where(head == z, 19, 20))

    colour = lax.rem(2 * (2 * xh + xl) + y, 4)

    def quarter(i, start=0, size=32):
        return pl.ds(pl.multiple_of(lax.rem(colour + i, 4) * 32 + start, 16), size)

    push(keys.at[z, xh, c, quarter(2)], keys.at[z, xh, c, quarter(2)], x_send.at[0], x_recv.at[0], across)
    push(keys.at[z, xh, c], keys.at[z, xh, c], c_send.at[0], c_recv.at[0], partner)
    for i in (0, 1, 3):
        ref = keys.at[z, xh, c, quarter(i)]
        remote(ref, ref, x_send.at[1], x_recv.at[1], across).start()

    factor = math.log2(math.e) / math.sqrt(NOPE + ROPE)
    for copy in loads:
        copy.wait()
    ahead = jnp.where((lane >= 64) & (lane - 64 > block_no) & (lane < 96), HIDDEN, 0.0)
    for h in range(HEADS):
        rows = pl.ds(h * ROWS, ROWS)
        folded = dot_nt(qn[:, h * NOPE : (h + 1) * NOPE], up[:, h * 256 : h * 256 + NOPE])
        query[rows, :KV_RANK] = folded.astype(BF16)
        turned = qr[:, h * ROPE : (h + 1) * ROPE].astype(F32)
        turned = jnp.concatenate([turned, jnp.zeros((ROWS, 64), F32)], axis=1)
        query[rows, KV_RANK:] = (turned + ahead).astype(BF16)
        if h == 1:
            landed(keys.at[z, 1 - xh, c, quarter(0)], x_send.at[0], x_recv.at[0])
            start = keys.at[z, :, c, quarter(0)]
            push(start, start, z_send.at[0, 0], z_recv.at[0, 0], right)
            push(start, start, z_send.at[1, 0], z_recv.at[1, 0], left)

    def w_piece(i):
        piece = pl.ds(pl.multiple_of((xh * 2 + c) * 224 + i * 32, 32), 32)
        remote(w_hbm.at[pl.ds(i * 32, 32)], w.at[piece], w_send.at[0], w_recv.at[0], opposite).start()

    def scores_of(k, i):
        return dot_nt(query[pl.ds(i * PART, PART), :], keys[slab(k)].reshape(512, WIDE))

    def absorb(k, i, scores):
        rows = pl.ds(i * PART, PART)
        if k == 0:
            own = xh * 256 + c * ROWS
            token = lax.rem(lax.broadcasted_iota(jnp.int32, (PART, 512), 0), ROWS)
            later = lax.broadcasted_iota(jnp.int32, (PART, 512), 1) - own
            scores = jnp.where((later > token) & (later < ROWS), HIDDEN, scores)
        most = jnp.max(scores, axis=1, keepdims=True)
        if k != 0:
            before = top[rows, :1]
            most = jnp.maximum(most, before)
            fade = jnp.exp2((before - most) * factor)
        expo = jnp.exp2((scores - most) * factor)
        mass = (expo[:, :128] + expo[:, 128:256]) + (expo[:, 256:384] + expo[:, 384:])
        values = keys[slab(k), :, :, :, :KV_RANK].reshape(512, KV_RANK)
        gained = jnp.dot(expo.astype(BF16), values, preferred_element_type=F32)
        if k == 0:
            summed[rows, :] = gained
            total[rows, :] = mass
        else:
            summed[rows, :] = summed[rows, :] * fade + gained
            total[rows, :] = total[rows, :] * fade + mass
        top[rows, :] = jnp.broadcast_to(most, (PART, 128))

    def attend(k):
        count = HEADS * ROWS // PART
        following = scores_of(k, 0)
        for i in range(count):
            scores = following
            if i + 1 < count:
                following = scores_of(k, i + 1)
            absorb(k, i, scores)

    slots = {-1: 0, 1: 1, -2: 2, 2: 3, -3: 4, 3: 5, 4: 6}

    def pass_on(k):
        i, block = slots[k], slab(k)
        mine = keys.at[block, :, c, quarter(0)]
        push(mine, mine, n_send.at[0, i], n_recv.at[0, i], above)
        push(mine, mine, n_send.at[1, i], n_recv.at[1, i], below)
        first, second = keys.at[block, :, c, quarter(0, 0, 16)], keys.at[block, :, c, quarter(0, 16, 16)]
        push(first, first, n_send.at[2, i], n_recv.at[2, i], beside)
        push(second, second, n_send.at[3, i], n_recv.at[3, i], across)

    def from_z(d):
        for k, way, forward in ((-d, 0, right), (d, 1, left)):
            if d < 4:
                ref = keys.at[slab(k), :, c, quarter(0)]
                landed(ref, z_send.at[way, d - 1], z_recv.at[way, d - 1])
                if d == 3:
                    ref = keys.at[slab(k), way, c, quarter(0)]
                push(ref, ref, z_send.at[way, d], z_recv.at[way, d], forward)
                pass_on(k)
            else:
                ref = keys.at[slab(4), way, c, quarter(0)]
                landed(ref, z_send.at[way, 3], z_recv.at[way, 3])
        if d == 4:
            pass_on(4)

    def from_plane(k):
        i, block = slots[k], slab(k)
        landed(keys.at[block, :, c, quarter(3)], n_send.at[0, i], n_recv.at[0, i])
        landed(keys.at[block, :, c, quarter(1)], n_send.at[1, i], n_recv.at[1, i])
        landed(keys.at[block, :, c, quarter(2, 0, 16)], n_send.at[2, i], n_recv.at[2, i])
        landed(keys.at[block, :, c, quarter(2, 16, 16)], n_send.at[3, i], n_recv.at[3, i])
        whole = keys.at[block, :, c]
        push(whole, whole, d_send.at[i], d_recv.at[i], partner)

    def ready(k):
        landed(keys.at[slab(k), :, 1 - c], d_send.at[slots[k]], d_recv.at[slots[k]])

    rest = keys.at[z, 1 - xh, c, pl.ds(0, 96)]
    landed(rest, x_send.at[1], x_recv.at[1])
    push(keys.at[z, 1 - xh, c], keys.at[z, 1 - xh, c], c_send.at[1], c_recv.at[1], partner)
    w_copy = load(w_hbm, w_own, 6)
    push(w_hbm, w_own, w_send.at[1], w_recv.at[1], partner)
    landed(keys.at[z, xh, 1 - c], c_send.at[0], c_recv.at[0])
    landed(keys.at[z, 1 - xh, 1 - c], c_send.at[1], c_recv.at[1])
    attend(0)
    from_z(1)
    w_piece(0)
    w_piece(1)
    from_z(2)
    w_piece(2)
    from_plane(-1)
    from_plane(1)
    ready(-1)
    attend(-1)
    from_z(3)
    w_piece(3)
    ready(1)
    attend(1)
    from_plane(-2)
    from_plane(2)
    ready(-2)
    attend(-2)
    from_z(4)
    w_piece(4)
    w_piece(5)
    w_piece(6)
    ready(2)
    attend(2)
    from_plane(-3)
    from_plane(3)
    ready(-3)
    attend(-3)
    from_plane(4)
    ready(3)
    attend(3)
    ready(4)
    attend(4)

    for p in (0, 1):
        for h in range(4 * p, 4 * p + 4):
            rows = pl.ds(h * ROWS, ROWS)
            share = summed[rows, :] / jnp.sum(total[rows, :], axis=1, keepdims=True)
            value = jnp.dot(share.astype(BF16), up[:, h * 256 + NOPE : (h + 1) * 256], preferred_element_type=F32)
            held[z, p, :, (h - 4 * p) * VDIM : (h - 4 * p + 1) * VDIM] = value.astype(BF16)
        ref = held.at[z, p]
        push(ref, ref, a_send.at[0, 0, p], a_recv.at[0, 0, p], right)
        push(ref, ref, a_send.at[1, 0, p], a_recv.at[1, 0, p], left)
    w_other = w.at[pl.ds(pl.multiple_of(((1 - xh) * 2 + c) * 224, 32), 224)]
    landed(w_other, w_send.at[0], w_recv.at[0])
    push(w_other, w_other, w_send.at[2], w_recv.at[2], partner)
    w_copy.wait()
    landed(w_other, w_send.at[1], w_recv.at[1])
    landed(w_other, w_send.at[2], w_recv.at[2])
    mine = pl.ds(pl.multiple_of(head * 16, 16), 16)

    def multiply(k):
        block = slab(k)
        product = dot_nt(held[block, 0], w[:, :512]) + dot_nt(held[block, 1], w[:, 512:])
        part[block] = product.astype(BF16)
        for j in range(1, 8):
            rows = pl.ds(pl.multiple_of(lax.rem(head + j, 8) * 16, 16), 16)
            remote(
                part.at[block, rows], reached.at[block, j - 1], s_send.at[block], s_recv.at[block], seat(z, head + j)
            ).start()

    def collect(k):
        block = slab(k)
        landed(reached.at[block], s_send.at[block], s_recv.at[block])
        acc = part[block, mine].astype(F32)
        for j in range(7):
            acc = acc + reached[block, j].astype(F32)
        done[block] = acc.astype(BF16)
        if k == 0:

            @pl.when(head == z)
            def _():
                pltpu.make_async_copy(done.at[block], final.at[mine], f_recv).start()

            @pl.when(head != z)
            def _():
                remote(done.at[block], final.at[mine], f_send.at[0], f_recv, seat(block, z)).start()
        else:
            push(done.at[block], final.at[mine], f_send.at[k + 3], f_recv, seat(block, z))

    multiply(0)
    for d in (1, 2, 3):
        for p in (0, 1):
            for k, way, forward in ((-d, 0, right), (d, 1, left)):
                ref = held.at[slab(k), p]
                landed(ref, a_send.at[way, d - 1, p], a_recv.at[way, d - 1, p])
                if d < 3 or p == way:
                    push(ref, ref, a_send.at[way, d, p], a_recv.at[way, d, p], forward)
        multiply(-d)
        multiply(d)
        if d == 1:
            collect(0)
        else:
            collect(1 - d)
            collect(d - 1)
    for way in (0, 1):
        landed(held.at[slab(4), way], a_send.at[way, 3, way], a_recv.at[way, 3, way])
    multiply(4)
    collect(-3)
    collect(3)
    collect(4)
    landed(final, f_send.at[0], f_recv)
    out_ref[...] = final[...]
    for copy in sent:
        copy.wait_send()
    remote(rest, rest, x_send.at[1], x_recv.at[1], across).wait_send()
    remote(w_other, w_other, w_send.at[0], w_recv.at[0], opposite).wait_send()
    for block in range(8):
        remote(reached.at[block], reached.at[block], s_send.at[block], s_recv.at[block], right).wait_send()

    @pl.when(head != z)
    def _():
        remote(done.at[0], done.at[0], f_send.at[0], f_recv, right).wait_send()


def local(q_nope, q_rope, kv_latent, positions, kv_gain, kv_up, w_out):
    dma = pltpu.SemaphoreType.DMA
    columns, depth = 4 * w_out.shape[1], w_out.shape[0]
    any_ = pl.BlockSpec(memory_space=pl.ANY)
    return pl.pallas_call(
        kernel,
        out_shape=jax.ShapeDtypeStruct((ROWS, columns), BF16),
        in_specs=[any_] * 7,
        out_specs=pl.BlockSpec(memory_space=pltpu.VMEM),
        scratch_shapes=[
            pltpu.SMEM((ROWS,), jnp.int32),
            pltpu.VMEM((KV_RANK + ROPE, ROWS), BF16),
            pltpu.VMEM((KV_RANK,), F32),
            pltpu.VMEM((8, 2, 2, ROWS, WIDE), BF16),
            pltpu.VMEM((ROWS, HEADS * NOPE), BF16),
            pltpu.VMEM((ROWS, HEADS * ROPE), BF16),
            pltpu.VMEM((KV_RANK, HEADS * 256), BF16),
            pltpu.VMEM((HEADS * ROWS, WIDE), BF16),
            pltpu.VMEM((HEADS * ROWS, 128), F32),
            pltpu.VMEM((HEADS * ROWS, 128), F32),
            pltpu.VMEM((HEADS * ROWS, KV_RANK), F32),
            pltpu.VMEM((8, 2, ROWS, depth // 2), BF16),
            pltpu.VMEM((columns, depth), BF16),
            pltpu.VMEM((8, ROWS, columns), BF16),
            pltpu.VMEM((8, 7, 16, columns), BF16),
            pltpu.VMEM((8, 16, columns), BF16),
            pltpu.VMEM((ROWS, columns), BF16),
            dma((7,)), dma((2,)), dma((2,)), dma((2,)), dma((2,)), dma((2, 4)), dma((2, 4)),
            dma((4, 7)), dma((4, 7)), dma((7,)), dma((7,)),
            dma((3,)), dma((3,)), dma((2, 4, 2)), dma((2, 4, 2)), dma((8,)), dma((8,)), dma((8,)), dma(()),
        ],
        compiler_params=pltpu.CompilerParams(
            collective_id=0, has_side_effects=True, vmem_limit_bytes=60 * 2**20
        ),
        cost_estimate=pl.CostEstimate(flops=13 * 10**9, bytes_accessed=4 * 10**6, transcendentals=4 * 10**6),
        name="attention",
    )(positions, kv_latent.T, kv_gain, q_nope, q_rope, kv_up, w_out.T)


def solution(mesh):
    return jax.shard_map(
        local,
        mesh=mesh,
        in_specs=(
            P("seq", "head"),
            P("seq", "head"),
            P("seq", None),
            P("seq"),
            P(),
            P(None, "head"),
            P("head", "seq"),
        ),
        out_specs=P("seq", "head"),
        check_vma=False,
    )
```

```python
import math

import jax
import jax.numpy as jnp
from jax import lax
from jax.experimental import pallas as pl
from jax.experimental.pallas import tpu as pltpu
from jax.sharding import PartitionSpec as P

KV_RANK = 512
ROPE = 64
NOPE = 128
VDIM = 128
ROWS = 128
HEADS = 8
WIDE = 640
PART = 256
HIDDEN = -1e30
MESH = pl.DeviceIdType.MESH
F32 = jnp.float32
BF16 = jnp.bfloat16


def dot_nt(a, b):
    return lax.dot_general(a, b, (((1,), (1,)), ((), ())), preferred_element_type=F32)


def kernel(
    pos_hbm, lat_hbm, gain_hbm, qn_hbm, qr_hbm, up_hbm, w_hbm, out_ref,
    pos_ref, lat_ref, gain_ref, keys, qn, qr, up, query, top, total, summed,
    held, w, part, reached, done, final,
    local_sem, x_send, x_recv, c_send, c_recv, z_send, z_recv, n_send, n_recv, d_send, d_recv,
    w_send, w_recv, a_send, a_recv, s_send, s_recv, f_send, f_recv,
):
    s, head = lax.axis_index("seq"), lax.axis_index("head")
    z, xh, c, xl, y = s // 4, lax.rem(s // 2, 2), lax.rem(s, 2), head // 4, lax.rem(head, 4)

    def at(z, xh, c, xl, y):
        return (lax.rem(z + 8, 8) * 4 + xh * 2 + c, xl * 4 + lax.rem(y + 4, 4))

    def seat(plane, col):
        return (lax.rem(plane, 8) * 4 + xh * 2 + c, lax.rem(col, 8))

    def slab(k):
        return lax.rem(z + k + 8, 8)

    across, beside = at(z, 1 - xh, c, 1 - xl, y), at(z, xh, c, 1 - xl, y)
    partner, opposite = at(z, xh, 1 - c, xl, y), at(z, 1 - xh, c, xl, y)
    right, left = at(z + 1, xh, c, xl, y), at(z - 1, xh, c, xl, y)
    above, below = at(z, xh, c, xl, y + 1), at(z, xh, c, xl, y - 1)

    def remote(src, dst, send, recv, peer):
        return pltpu.make_async_remote_copy(
            src_ref=src, dst_ref=dst, send_sem=send, recv_sem=recv, device_id=peer, device_id_type=MESH
        )

    sent = []

    def push(src, dst, send, recv, peer):
        copy = remote(src, dst, send, recv, peer)
        copy.start()
        sent.append(copy)

    def landed(ref, send, recv):
        remote(ref, ref, send, recv, partner).wait_recv()

    def load(src, dst, i):
        copy = pltpu.make_async_copy(src, dst, local_sem.at[i])
        copy.start()
        return copy

    w_own = w.at[pl.ds(pl.multiple_of((xh * 2 + c) * 224, 32), 224)]
    first_loads = [load(lat_hbm, lat_ref, 0), load(gain_hbm, gain_ref, 1), load(pos_hbm, pos_ref, 2)]
    loads = [load(qn_hbm, qn, 3), load(up_hbm, up, 4), load(qr_hbm, qr, 5)]

    barrier = pltpu.get_barrier_semaphore()

    def greet(peer):
        pl.semaphore_signal(barrier, inc=1, device_id=peer, device_id_type=MESH)

    for peer in (across, partner, opposite, right, left, at(z + 1, 1 - xh, c, 1 - xl, y), at(z - 1, 1 - xh, c, 1 - xl, y)):
        greet(peer)
    for j in range(1, 8):
        greet(seat(z, head + j))
    for j in range(8):
        pl.when((head != z) | (head != j))(lambda: greet(seat(head, j)))

    for copy in first_loads:
        copy.wait()
    block_no = pos_ref[0] // ROWS
    lane = lax.broadcasted_iota(jnp.int32, (ROWS, 128), 1)
    coded = lat_ref[:KV_RANK, :].astype(F32).T
    latent = coded * lax.rsqrt(jnp.mean(coded * coded, axis=1, keepdims=True) + 1e-06)
    keys[z, xh, c, :, :KV_RANK] = (latent * gain_ref[...].reshape(1, KV_RANK)).astype(BF16)
    rope = lat_ref[KV_RANK:, :].astype(F32)
    tail = jnp.concatenate([rope, jnp.zeros((64, ROWS), F32)], axis=0).T
    keys[z, xh, c, :, KV_RANK:] = jnp.where(lane == 64 + block_no, 1.0, tail).astype(BF16)
    pl.semaphore_wait(barrier, jnp.where(head == z, 21, 22))

    colour = lax.rem(2 * (2 * xh + xl) + y, 4)

    def quarter(i, start=0, size=32):
        return pl.ds(pl.multiple_of(lax.rem(colour + i, 4) * 32 + start, 16), size)

    first, second = keys.at[z, xh, c, quarter(0)], keys.at[z, xh, c, quarter(2)]
    for way, step in ((0, 1), (1, -1)):
        push(first, first, z_send.at[way, 0, 0], z_recv.at[way, 0, 0], at(z + step, xh, c, xl, y))
        push(second, second, z_send.at[way, 0, 1], z_recv.at[way, 0, 1], at(z + step, 1 - xh, c, 1 - xl, y))
    push(keys.at[z, xh, c], keys.at[z, xh, c], x_send.at[0], x_recv.at[0], across)
    push(keys.at[z, xh, c], keys.at[z, xh, c], c_send.at[0], c_recv.at[0], partner)

    factor = math.log2(math.e) / math.sqrt(NOPE + ROPE)
    for copy in loads:
        copy.wait()
    ahead = jnp.where((lane >= 64) & (lane - 64 > block_no) & (lane < 96), HIDDEN, 0.0)

    def fold(h):
        rows = pl.ds(h * ROWS, ROWS)
        folded = dot_nt(qn[:, h * NOPE : (h + 1) * NOPE], up[:, h * 256 : h * 256 + NOPE])
        query[rows, :KV_RANK] = folded.astype(BF16)
        turned = qr[:, h * ROPE : (h + 1) * ROPE].astype(F32)
        turned = jnp.concatenate([turned, jnp.zeros((ROWS, 64), F32)], axis=1)
        query[rows, KV_RANK:] = (turned + ahead).astype(BF16)

    for h in range(4):
        fold(h)

    def w_piece(i):
        piece = pl.ds(pl.multiple_of((xh * 2 + c) * 224 + i * 32, 32), 32)
        remote(w_hbm.at[pl.ds(i * 32, 32)], w.at[piece], w_send.at[0], w_recv.at[0], opposite).start()

    def scores_of(k, i):
        return dot_nt(query[pl.ds(i * PART, PART), :], keys[slab(k)].reshape(512, WIDE))

    def absorb(k, i, scores):
        rows = pl.ds(i * PART, PART)
        if k == 0:
            own = xh * 256 + c * ROWS
            token = lax.rem(lax.broadcasted_iota(jnp.int32, (PART, 512), 0), ROWS)
            later = lax.broadcasted_iota(jnp.int32, (PART, 512), 1) - own
            scores = jnp.where((later > token) & (later < ROWS), HIDDEN, scores)
        most = jnp.max(scores, axis=1, keepdims=True)
        if k != 0:
            before = top[rows, :1]
            most = jnp.maximum(most, before)
            fade = jnp.exp2((before - most) * factor)
        expo = jnp.exp2((scores - most) * factor)
        mass = (expo[:, :128] + expo[:, 128:256]) + (expo[:, 256:384] + expo[:, 384:])
        values = keys[slab(k), :, :, :, :KV_RANK].reshape(512, KV_RANK)
        gained = jnp.dot(expo.astype(BF16), values, preferred_element_type=F32)
        if k == 0:
            summed[rows, :] = gained
            total[rows, :] = mass
        else:
            summed[rows, :] = summed[rows, :] * fade + gained
            total[rows, :] = total[rows, :] * fade + mass
        top[rows, :] = jnp.broadcast_to(most, (PART, 128))

    def attend(k, finish=None):
        count = HEADS * ROWS // PART
        following = scores_of(k, 0)
        for i in range(count):
            scores = following
            if i + 1 < count:
                following = scores_of(k, i + 1)
            absorb(k, i, scores)
            if finish is not None and (i + 1) % (count // 2) == 0:
                finish((i + 1) // (count // 2) - 1)

    slots = {-1: 0, 1: 1, -2: 2, 2: 3, -3: 4, 3: 5, 4: 6}

    def pass_on(k):
        i, block = slots[k], slab(k)
        mine = keys.at[block, :, c, quarter(0)]
        push(mine, mine, n_send.at[0, i], n_recv.at[0, i], above)
        push(mine, mine, n_send.at[1, i], n_recv.at[1, i], below)
        first, second = keys.at[block, :, c, quarter(0, 0, 16)], keys.at[block, :, c, quarter(0, 16, 16)]
        push(first, first, n_send.at[2, i], n_recv.at[2, i], beside)
        push(second, second, n_send.at[3, i], n_recv.at[3, i], across)

    def from_z(d):
        for t in (0, 1):
            kind = xh if t == 0 else 1 - xh
            for k, way, forward in ((-d, 0, right), (d, 1, left)):
                ref = keys.at[slab(k), kind, c, quarter(0)]
                if d < 4 or t == way:
                    landed(ref, z_send.at[way, d - 1, t], z_recv.at[way, d - 1, t])
                if d < 3 or (d == 3 and t == way):
                    push(ref, ref, z_send.at[way, d, t], z_recv.at[way, d, t], forward)
        for k in (-d, d) if d < 4 else (4,):
            pass_on(k)

    def from_plane(k):
        i, block = slots[k], slab(k)
        landed(keys.at[block, :, c, quarter(3)], n_send.at[0, i], n_recv.at[0, i])
        landed(keys.at[block, :, c, quarter(1)], n_send.at[1, i], n_recv.at[1, i])
        landed(keys.at[block, :, c, quarter(2, 0, 16)], n_send.at[2, i], n_recv.at[2, i])
        landed(keys.at[block, :, c, quarter(2, 16, 16)], n_send.at[3, i], n_recv.at[3, i])
        whole = keys.at[block, :, c]
        push(whole, whole, d_send.at[i], d_recv.at[i], partner)

    def ready(k):
        landed(keys.at[slab(k), :, 1 - c], d_send.at[slots[k]], d_recv.at[slots[k]])

    from_z(1)
    for h in range(4, 8):
        fold(h)
    from_z(2)
    theirs = keys.at[z, 1 - xh, c]
    landed(theirs, x_send.at[0], x_recv.at[0])
    push(theirs, theirs, c_send.at[1], c_recv.at[1], partner)
    w_copy = load(w_hbm, w_own, 6)
    w_piece(0)
    from_z(3)
    from_plane(-1)
    from_plane(1)
    landed(keys.at[z, xh, 1 - c], c_send.at[0], c_recv.at[0])
    landed(keys.at[z, 1 - xh, 1 - c], c_send.at[1], c_recv.at[1])
    attend(0)
    from_z(4)
    w_piece(1)
    w_piece(2)
    w_piece(3)
    from_plane(-2)
    ready(-1)
    attend(-1)
    from_plane(2)
    w_piece(4)
    w_piece(5)
    w_piece(6)
    push(w_hbm, w_own, w_send.at[1], w_recv.at[1], partner)
    ready(1)
    attend(1)
    from_plane(-3)
    ready(-2)
    attend(-2)
    from_plane(3)
    ready(2)
    attend(2)
    from_plane(4)
    ready(-3)
    attend(-3)
    ready(3)
    attend(3)
    ready(4)

    def finish(p):
        for h in range(4 * p, 4 * p + 4):
            rows = pl.ds(h * ROWS, ROWS)
            share = summed[rows, :] / jnp.sum(total[rows, :], axis=1, keepdims=True)
            value = jnp.dot(share.astype(BF16), up[:, h * 256 + NOPE : (h + 1) * 256], preferred_element_type=F32)
            held[z, p, :, (h - 4 * p) * VDIM : (h - 4 * p + 1) * VDIM] = value.astype(BF16)
        ref = held.at[z, p]
        push(ref, ref, a_send.at[0, 0, p], a_recv.at[0, 0, p], right)
        push(ref, ref, a_send.at[1, 0, p], a_recv.at[1, 0, p], left)

    attend(4, finish)

    earlier = sent[:-4]
    del sent[:-4]

    def flush(copies):
        for copy in copies:
            copy.wait_send()

    w_other = w.at[pl.ds(pl.multiple_of(((1 - xh) * 2 + c) * 224, 32), 224)]
    landed(w_other, w_send.at[0], w_recv.at[0])
    push(w_other, w_other, w_send.at[2], w_recv.at[2], partner)
    w_copy.wait()
    landed(w_other, w_send.at[1], w_recv.at[1])
    landed(w_other, w_send.at[2], w_recv.at[2])
    mine = pl.ds(pl.multiple_of(head * 16, 16), 16)

    def multiply(k):
        block = slab(k)
        product = dot_nt(held[block, 0], w[:, :512]) + dot_nt(held[block, 1], w[:, 512:])
        part[block] = product.astype(BF16)
        for j in range(1, 8):
            rows = pl.ds(pl.multiple_of(lax.rem(head + j, 8) * 16, 16), 16)
            remote(
                part.at[block, rows], reached.at[block, j - 1], s_send.at[block], s_recv.at[block], seat(z, head + j)
            ).start()

    def collect(k):
        block = slab(k)
        landed(reached.at[block], s_send.at[block], s_recv.at[block])
        acc = part[block, mine].astype(F32)
        for j in range(7):
            acc = acc + reached[block, j].astype(F32)
        done[block] = acc.astype(BF16)
        if k == 0:

            @pl.when(head == z)
            def _():
                pltpu.make_async_copy(done.at[block], final.at[mine], f_recv).start()

            @pl.when(head != z)
            def _():
                remote(done.at[block], final.at[mine], f_send.at[0], f_recv, seat(block, z)).start()
        else:
            push(done.at[block], final.at[mine], f_send.at[k + 3], f_recv, seat(block, z))

    def from_ring(d, p):
        for k, way, forward in ((-d, 0, right), (d, 1, left)):
            ref = held.at[slab(k), p]
            landed(ref, a_send.at[way, d - 1, p], a_recv.at[way, d - 1, p])
            if d < 3 or p == way:
                push(ref, ref, a_send.at[way, d, p], a_recv.at[way, d, p], forward)

    multiply(0)
    flush(earlier)
    remote(w_other, w_other, w_send.at[0], w_recv.at[0], opposite).wait_send()
    from_ring(1, 0)
    from_ring(1, 1)
    multiply(-1)
    multiply(1)
    from_ring(2, 0)
    collect(0)
    from_ring(2, 1)
    multiply(-2)
    multiply(2)
    from_ring(3, 0)
    collect(-1)
    collect(1)
    from_ring(3, 1)
    multiply(-3)
    multiply(3)
    collect(-2)
    collect(2)
    for way in (0, 1):
        landed(held.at[slab(4), way], a_send.at[way, 3, way], a_recv.at[way, 3, way])
    multiply(4)
    flush(sent)
    sent.clear()
    for k in (0, -1, 1, -2, 2):
        remote(reached.at[slab(k)], reached.at[slab(k)], s_send.at[slab(k)], s_recv.at[slab(k)], right).wait_send()
    collect(-3)
    collect(3)
    collect(4)
    for k in (-3, 3, 4):
        remote(reached.at[slab(k)], reached.at[slab(k)], s_send.at[slab(k)], s_recv.at[slab(k)], right).wait_send()
    flush(sent)

    @pl.when(head != z)
    def _():
        remote(done.at[0], done.at[0], f_send.at[0], f_recv, right).wait_send()

    landed(final, f_send.at[0], f_recv)
    out_ref[...] = final[...]


def local(q_nope, q_rope, kv_latent, positions, kv_gain, kv_up, w_out):
    dma = pltpu.SemaphoreType.DMA
    columns, depth = 4 * w_out.shape[1], w_out.shape[0]
    any_ = pl.BlockSpec(memory_space=pl.ANY)
    return pl.pallas_call(
        kernel,
        out_shape=jax.ShapeDtypeStruct((ROWS, columns), BF16),
        in_specs=[any_] * 7,
        out_specs=pl.BlockSpec(memory_space=pltpu.VMEM),
        scratch_shapes=[
            pltpu.SMEM((ROWS,), jnp.int32),
            pltpu.VMEM((KV_RANK + ROPE, ROWS), BF16),
            pltpu.VMEM((KV_RANK,), F32),
            pltpu.VMEM((8, 2, 2, ROWS, WIDE), BF16),
            pltpu.VMEM((ROWS, HEADS * NOPE), BF16),
            pltpu.VMEM((ROWS, HEADS * ROPE), BF16),
            pltpu.VMEM((KV_RANK, HEADS * 256), BF16),
            pltpu.VMEM((HEADS * ROWS, WIDE), BF16),
            pltpu.VMEM((HEADS * ROWS, 128), F32),
            pltpu.VMEM((HEADS * ROWS, 128), F32),
            pltpu.VMEM((HEADS * ROWS, KV_RANK), F32),
            pltpu.VMEM((8, 2, ROWS, depth // 2), BF16),
            pltpu.VMEM((columns, depth), BF16),
            pltpu.VMEM((8, ROWS, columns), BF16),
            pltpu.VMEM((8, 7, 16, columns), BF16),
            pltpu.VMEM((8, 16, columns), BF16),
            pltpu.VMEM((ROWS, columns), BF16),
            dma((7,)), dma((1,)), dma((1,)), dma((2,)), dma((2,)), dma((2, 4, 2)), dma((2, 4, 2)),
            dma((4, 7)), dma((4, 7)), dma((7,)), dma((7,)),
            dma((3,)), dma((3,)), dma((2, 4, 2)), dma((2, 4, 2)),
            dma((8,)), dma((8,)), dma((8,)), dma(()),
        ],
        compiler_params=pltpu.CompilerParams(
            collective_id=0, has_side_effects=True, vmem_limit_bytes=60 * 2**20
        ),
        cost_estimate=pl.CostEstimate(flops=13 * 10**9, bytes_accessed=4 * 10**6, transcendentals=4 * 10**6),
        name="attention",
    )(positions, kv_latent.T, kv_gain, q_nope, q_rope, kv_up, w_out.T)


def solution(mesh):
    return jax.shard_map(
        local,
        mesh=mesh,
        in_specs=(
            P("seq", "head"),
            P("seq", "head"),
            P("seq", None),
            P("seq"),
            P(),
            P(None, "head"),
            P("head", "seq"),
        ),
        out_specs=P("seq", "head"),
        check_vma=False,
    )
```

```python
import math

import jax
import jax.numpy as jnp
from jax import lax
from jax.experimental import pallas as pl
from jax.experimental.pallas import tpu as pltpu
from jax.sharding import PartitionSpec as P

KV_RANK = 512
ROPE = 64
NOPE = 128
VDIM = 128
ROWS = 128
HEADS = 8
WIDE = 640
PART = 256
HIDDEN = -1e30
MESH = pl.DeviceIdType.MESH
F32 = jnp.float32
BF16 = jnp.bfloat16


def dot_nt(a, b):
    return lax.dot_general(a, b, (((1,), (1,)), ((), ())), preferred_element_type=F32)


def kernel(
    pos_hbm, lat_hbm, gain_hbm, qn_hbm, qr_hbm, up_hbm, w_hbm, out_ref,
    pos_ref, lat_ref, gain_ref, keys, qn, qr, up, query, top, total, summed,
    held, w, part, half, strips, sums, reached, done, final,
    local_sem, x_send, x_recv, c_send, c_recv, z_send, z_recv, n_send, n_recv, d_send, d_recv,
    w_send, w_recv, a_send, a_recv, p_send, p_recv, s_send, s_recv, f_send, f_recv,
):
    s, head = lax.axis_index("seq"), lax.axis_index("head")
    z, xh, c, xl, y = s // 4, lax.rem(s // 2, 2), lax.rem(s, 2), head // 4, lax.rem(head, 4)

    def at(z, xh, c, xl, y):
        return (lax.rem(z + 8, 8) * 4 + xh * 2 + c, xl * 4 + lax.rem(y + 4, 4))

    def seat(plane, col):
        return (lax.rem(plane, 8) * 4 + xh * 2 + c, lax.rem(col, 8))

    def slab(k):
        return lax.rem(z + k + 8, 8)

    across, beside = at(z, 1 - xh, c, 1 - xl, y), at(z, xh, c, 1 - xl, y)
    partner, opposite = at(z, xh, 1 - c, xl, y), at(z, 1 - xh, c, xl, y)
    right, left = at(z + 1, xh, c, xl, y), at(z - 1, xh, c, xl, y)
    above, below = at(z, xh, c, xl, y + 1), at(z, xh, c, xl, y - 1)

    def remote(src, dst, send, recv, peer):
        return pltpu.make_async_remote_copy(
            src_ref=src, dst_ref=dst, send_sem=send, recv_sem=recv, device_id=peer, device_id_type=MESH
        )

    sent = []

    def push(src, dst, send, recv, peer):
        copy = remote(src, dst, send, recv, peer)
        copy.start()
        sent.append(copy)

    def landed(ref, send, recv):
        remote(ref, ref, send, recv, partner).wait_recv()

    def load(src, dst, i):
        copy = pltpu.make_async_copy(src, dst, local_sem.at[i])
        copy.start()
        return copy

    w_own = w.at[pl.ds(pl.multiple_of((xh * 2 + c) * 224, 32), 224)]
    first_loads = [load(lat_hbm, lat_ref, 0), load(gain_hbm, gain_ref, 1), load(pos_hbm, pos_ref, 2)]
    loads = [load(qn_hbm, qn, 3), load(up_hbm, up, 4), load(qr_hbm, qr, 5)]

    barrier = pltpu.get_barrier_semaphore()

    def greet(peer):
        pl.semaphore_signal(barrier, inc=1, device_id=peer, device_id_type=MESH)

    for peer in (across, partner, opposite, right, left, at(z + 1, 1 - xh, c, 1 - xl, y), at(z - 1, 1 - xh, c, 1 - xl, y)):
        greet(peer)
    for j in range(1, 8):
        greet(seat(z, head + j))
    for j in range(8):
        pl.when((head != z) | (head != j))(lambda: greet(seat(head, j)))

    for copy in first_loads:
        copy.wait()
    block_no = pos_ref[0] // ROWS
    lane = lax.broadcasted_iota(jnp.int32, (ROWS, 128), 1)
    coded = lat_ref[:KV_RANK, :].astype(F32).T
    latent = coded * lax.rsqrt(jnp.mean(coded * coded, axis=1, keepdims=True) + 1e-06)
    keys[z, xh, c, :, :KV_RANK] = (latent * gain_ref[...].reshape(1, KV_RANK)).astype(BF16)
    rope = lat_ref[KV_RANK:, :].astype(F32)
    tail = jnp.concatenate([rope, jnp.zeros((64, ROWS), F32)], axis=0).T
    keys[z, xh, c, :, KV_RANK:] = jnp.where(lane == 64 + block_no, 1.0, tail).astype(BF16)
    pl.semaphore_wait(barrier, jnp.where(head == z, 21, 22))

    colour = lax.rem(2 * (2 * xh + xl) + y, 4)

    def quarter(i, start=0, size=32):
        return pl.ds(pl.multiple_of(lax.rem(colour + i, 4) * 32 + start, 16), size)

    first, second = keys.at[z, xh, c, quarter(0)], keys.at[z, xh, c, quarter(2)]
    for way, step in ((0, 1), (1, -1)):
        push(first, first, z_send.at[way, 0, 0], z_recv.at[way, 0, 0], at(z + step, xh, c, xl, y))
        push(second, second, z_send.at[way, 0, 1], z_recv.at[way, 0, 1], at(z + step, 1 - xh, c, 1 - xl, y))
    push(keys.at[z, xh, c], keys.at[z, xh, c], x_send.at[0], x_recv.at[0], across)
    push(keys.at[z, xh, c], keys.at[z, xh, c], c_send.at[0], c_recv.at[0], partner)

    factor = math.log2(math.e) / math.sqrt(NOPE + ROPE)
    for copy in loads:
        copy.wait()
    ahead = jnp.where((lane >= 64) & (lane - 64 > block_no) & (lane < 96), HIDDEN, 0.0)

    def fold(h):
        rows = pl.ds(h * ROWS, ROWS)
        folded = dot_nt(qn[:, h * NOPE : (h + 1) * NOPE], up[:, h * 256 : h * 256 + NOPE])
        query[rows, :KV_RANK] = folded.astype(BF16)
        turned = qr[:, h * ROPE : (h + 1) * ROPE].astype(F32)
        turned = jnp.concatenate([turned, jnp.zeros((ROWS, 64), F32)], axis=1)
        query[rows, KV_RANK:] = (turned + ahead).astype(BF16)

    for h in range(4):
        fold(h)

    def w_piece(i):
        piece = pl.ds(pl.multiple_of((xh * 2 + c) * 224 + i * 32, 32), 32)
        remote(w_hbm.at[pl.ds(i * 32, 32)], w.at[piece], w_send.at[0], w_recv.at[0], opposite).start()

    def scores_of(k, i):
        return dot_nt(query[pl.ds(i * PART, PART), :], keys[slab(k)].reshape(512, WIDE))

    def absorb(k, i, scores):
        rows = pl.ds(i * PART, PART)
        if k == 0:
            own = xh * 256 + c * ROWS
            token = lax.rem(lax.broadcasted_iota(jnp.int32, (PART, 512), 0), ROWS)
            later = lax.broadcasted_iota(jnp.int32, (PART, 512), 1) - own
            scores = jnp.where((later > token) & (later < ROWS), HIDDEN, scores)
        most = jnp.max(scores, axis=1, keepdims=True)
        if k != 0:
            before = top[rows, :1]
            most = jnp.maximum(most, before)
            fade = jnp.exp2((before - most) * factor)
        expo = jnp.exp2((scores - most) * factor)
        mass = (expo[:, :128] + expo[:, 128:256]) + (expo[:, 256:384] + expo[:, 384:])
        values = keys[slab(k), :, :, :, :KV_RANK].reshape(512, KV_RANK)
        gained = jnp.dot(expo.astype(BF16), values, preferred_element_type=F32)
        if k == 0:
            summed[rows, :] = gained
            total[rows, :] = mass
        else:
            summed[rows, :] = summed[rows, :] * fade + gained
            total[rows, :] = total[rows, :] * fade + mass
        top[rows, :] = jnp.broadcast_to(most, (PART, 128))

    def attend(k, finish=None):
        count = HEADS * ROWS // PART
        following = scores_of(k, 0)
        for i in range(count):
            scores = following
            if i + 1 < count:
                following = scores_of(k, i + 1)
            absorb(k, i, scores)
            if finish is not None and (i + 1) % (count // 2) == 0:
                finish((i + 1) // (count // 2) - 1)

    slots = {-1: 0, 1: 1, -2: 2, 2: 3, -3: 4, 3: 5, 4: 6}

    def pass_on(k):
        i, block = slots[k], slab(k)
        mine = keys.at[block, :, c, quarter(0)]
        push(mine, mine, n_send.at[0, i], n_recv.at[0, i], above)
        push(mine, mine, n_send.at[1, i], n_recv.at[1, i], below)
        first, second = keys.at[block, :, c, quarter(0, 0, 16)], keys.at[block, :, c, quarter(0, 16, 16)]
        push(first, first, n_send.at[2, i], n_recv.at[2, i], beside)
        push(second, second, n_send.at[3, i], n_recv.at[3, i], across)

    def from_z(d):
        for t in (0, 1):
            kind = xh if t == 0 else 1 - xh
            for k, way, forward in ((-d, 0, right), (d, 1, left)):
                ref = keys.at[slab(k), kind, c, quarter(0)]
                if d < 4 or t == way:
                    landed(ref, z_send.at[way, d - 1, t], z_recv.at[way, d - 1, t])
                if d < 3 or (d == 3 and t == way):
                    push(ref, ref, z_send.at[way, d, t], z_recv.at[way, d, t], forward)
        for k in (-d, d) if d < 4 else (4,):
            pass_on(k)

    def from_plane(k):
        i, block = slots[k], slab(k)
        landed(keys.at[block, :, c, quarter(3)], n_send.at[0, i], n_recv.at[0, i])
        landed(keys.at[block, :, c, quarter(1)], n_send.at[1, i], n_recv.at[1, i])
        landed(keys.at[block, :, c, quarter(2, 0, 16)], n_send.at[2, i], n_recv.at[2, i])
        landed(keys.at[block, :, c, quarter(2, 16, 16)], n_send.at[3, i], n_recv.at[3, i])
        whole = keys.at[block, :, c]
        push(whole, whole, d_send.at[i], d_recv.at[i], partner)

    def ready(k):
        landed(keys.at[slab(k), :, 1 - c], d_send.at[slots[k]], d_recv.at[slots[k]])

    from_z(1)
    for h in range(4, 8):
        fold(h)
    from_z(2)
    theirs = keys.at[z, 1 - xh, c]
    landed(theirs, x_send.at[0], x_recv.at[0])
    push(theirs, theirs, c_send.at[1], c_recv.at[1], partner)
    w_copy = load(w_hbm, w_own, 6)
    w_piece(0)
    from_z(3)
    from_plane(-1)
    from_plane(1)
    landed(keys.at[z, xh, 1 - c], c_send.at[0], c_recv.at[0])
    landed(keys.at[z, 1 - xh, 1 - c], c_send.at[1], c_recv.at[1])
    attend(0)
    from_z(4)
    w_piece(1)
    w_piece(2)
    w_piece(3)
    from_plane(-2)
    ready(-1)
    attend(-1)
    from_plane(2)
    w_piece(4)
    w_piece(5)
    w_piece(6)
    push(w_hbm, w_own, w_send.at[1], w_recv.at[1], partner)
    ready(1)
    attend(1)
    from_plane(-3)
    ready(-2)
    attend(-2)
    from_plane(3)
    ready(2)
    attend(2)
    from_plane(4)
    ready(-3)
    attend(-3)
    ready(3)
    attend(3)
    ready(4)

    def finish(p):
        for h in range(4 * p, 4 * p + 4):
            rows = pl.ds(h * ROWS, ROWS)
            share = summed[rows, :] / jnp.sum(total[rows, :], axis=1, keepdims=True)
            value = jnp.dot(share.astype(BF16), up[:, h * 256 + NOPE : (h + 1) * 256], preferred_element_type=F32)
            held[z, p, :, (h - 4 * p) * VDIM : (h - 4 * p + 1) * VDIM] = value.astype(BF16)
        ref = held.at[z, p]
        push(ref, ref, a_send.at[0, 0, p], a_recv.at[0, 0, p], right)
        push(ref, ref, a_send.at[1, 0, p], a_recv.at[1, 0, p], left)

    attend(4, finish)

    earlier = sent[:-4]
    del sent[:-4]

    def flush(copies):
        for copy in copies:
            copy.wait_send()

    w_other = w.at[pl.ds(pl.multiple_of(((1 - xh) * 2 + c) * 224, 32), 224)]
    landed(w_other, w_send.at[0], w_recv.at[0])
    push(w_other, w_other, w_send.at[2], w_recv.at[2], partner)
    w_copy.wait()
    landed(w_other, w_send.at[1], w_recv.at[1])
    landed(w_other, w_send.at[2], w_recv.at[2])
    mine = pl.ds(pl.multiple_of(head * 16, 16), 16)

    lot = pl.ds(pl.multiple_of(y * 16, 16), 16)

    def lot_of(j):
        return pl.ds(pl.multiple_of(lax.rem(y + j, 4) * 16, 16), 16)

    def multiply(k):
        block = slab(k)
        product = dot_nt(held[block, 0], w[:, :512]) + dot_nt(held[block, 1], w[:, 512:])
        part[block] = product.astype(BF16).reshape(2, 64, product.shape[1])
        if k == -3:
            push(part.at[block, 1 - xl], half, p_send.at[0], p_recv.at[0], beside)
        elif k == 3:
            for j in (1, 2, 3):
                remote(
                    part.at[block, :, lot_of(j)], strips.at[j - 1], p_send.at[1], p_recv.at[1], at(z, xh, c, xl, y + j)
                ).start()
        else:
            for j in range(1, 8):
                t = lax.rem(head + j, 8)
                rows = pl.ds(pl.multiple_of(lax.rem(t, 4) * 16, 16), 16)
                remote(
                    part.at[block, t // 4, rows], reached.at[block, j - 1], s_send.at[block], s_recv.at[block], seat(z, t)
                ).start()

    def relay(k):
        block = slab(k)
        if k == -3:
            landed(half, p_send.at[0], p_recv.at[0])
            half[...] = (part[block, xl].astype(F32) + half[...].astype(F32)).astype(BF16)
            for j in (1, 2, 3):
                remote(
                    half.at[lot_of(j)], reached.at[block, j - 1], s_send.at[block], s_recv.at[block],
                    at(z, xh, c, xl, y + j),
                ).start()
        else:
            landed(strips, p_send.at[1], p_recv.at[1])
            acc = part[block, :, lot].astype(F32)
            for j in range(3):
                acc = acc + strips[j].astype(F32)
            sums[...] = acc.astype(BF16)
            push(sums.at[1 - xl], reached.at[block, 0], s_send.at[block], s_recv.at[block], beside)

    def collect(k):
        block = slab(k)
        pieces = {-3: 3, 3: 1}.get(k, 7)
        landed(reached.at[block, pl.ds(0, pieces)], s_send.at[block], s_recv.at[block])
        if k == -3:
            acc = half[lot].astype(F32)
        elif k == 3:
            acc = sums[xl].astype(F32)
        else:
            acc = part[block, xl, lot].astype(F32)
        for j in range(pieces):
            acc = acc + reached[block, j].astype(F32)
        done[block] = acc.astype(BF16)
        if k == 0:

            @pl.when(head == z)
            def _():
                pltpu.make_async_copy(done.at[block], final.at[mine], f_recv).start()

            @pl.when(head != z)
            def _():
                remote(done.at[block], final.at[mine], f_send.at[0], f_recv, seat(block, z)).start()
        else:
            push(done.at[block], final.at[mine], f_send.at[k + 3], f_recv, seat(block, z))

    def from_ring(d, p):
        for k, way, forward in ((-d, 0, right), (d, 1, left)):
            ref = held.at[slab(k), p]
            landed(ref, a_send.at[way, d - 1, p], a_recv.at[way, d - 1, p])
            if d < 3 or p == way:
                push(ref, ref, a_send.at[way, d, p], a_recv.at[way, d, p], forward)

    multiply(0)
    flush(earlier)
    remote(w_other, w_other, w_send.at[0], w_recv.at[0], opposite).wait_send()
    from_ring(1, 0)
    from_ring(1, 1)
    multiply(-1)
    multiply(1)
    from_ring(2, 0)
    collect(0)
    from_ring(2, 1)
    multiply(-2)
    multiply(2)
    from_ring(3, 0)
    collect(-1)
    collect(1)
    from_ring(3, 1)
    multiply(-3)
    multiply(3)
    collect(-2)
    collect(2)
    for way in (0, 1):
        landed(held.at[slab(4), way], a_send.at[way, 3, way], a_recv.at[way, 3, way])
    multiply(4)
    relay(-3)
    relay(3)
    collect(4)
    collect(-3)
    collect(3)
    for k in (0, -1, 1, -2, 2):
        remote(reached.at[slab(k)], reached.at[slab(k)], s_send.at[slab(k)], s_recv.at[slab(k)], right).wait_send()
    pieces = reached.at[slab(-3), pl.ds(0, 3)]
    remote(pieces, pieces, s_send.at[slab(-3)], s_recv.at[slab(-3)], right).wait_send()
    remote(strips, strips, p_send.at[1], p_recv.at[1], right).wait_send()
    for k in (4,):
        remote(reached.at[slab(k)], reached.at[slab(k)], s_send.at[slab(k)], s_recv.at[slab(k)], right).wait_send()
    flush(sent)

    @pl.when(head != z)
    def _():
        remote(done.at[0], done.at[0], f_send.at[0], f_recv, right).wait_send()

    landed(final, f_send.at[0], f_recv)
    out_ref[...] = final[...]


def local(q_nope, q_rope, kv_latent, positions, kv_gain, kv_up, w_out):
    dma = pltpu.SemaphoreType.DMA
    columns, depth = 4 * w_out.shape[1], w_out.shape[0]
    any_ = pl.BlockSpec(memory_space=pl.ANY)
    return pl.pallas_call(
        kernel,
        out_shape=pltpu.VMEM((ROWS, columns), BF16),
        in_specs=[any_] * 7,
        out_specs=pl.BlockSpec(memory_space=pltpu.VMEM),
        scratch_shapes=[
            pltpu.SMEM((ROWS,), jnp.int32),
            pltpu.VMEM((KV_RANK + ROPE, ROWS), BF16),
            pltpu.VMEM((KV_RANK,), F32),
            pltpu.VMEM((8, 2, 2, ROWS, WIDE), BF16),
            pltpu.VMEM((ROWS, HEADS * NOPE), BF16),
            pltpu.VMEM((ROWS, HEADS * ROPE), BF16),
            pltpu.VMEM((KV_RANK, HEADS * 256), BF16),
            pltpu.VMEM((HEADS * ROWS, WIDE), BF16),
            pltpu.VMEM((HEADS * ROWS, 128), F32),
            pltpu.VMEM((HEADS * ROWS, 128), F32),
            pltpu.VMEM((HEADS * ROWS, KV_RANK), F32),
            pltpu.VMEM((8, 2, ROWS, depth // 2), BF16),
            pltpu.VMEM((columns, depth), BF16),
            pltpu.VMEM((8, 2, 64, columns), BF16),
            pltpu.VMEM((64, columns), BF16),
            pltpu.VMEM((3, 2, 16, columns), BF16),
            pltpu.VMEM((2, 16, columns), BF16),
            pltpu.VMEM((8, 7, 16, columns), BF16),
            pltpu.VMEM((8, 16, columns), BF16),
            pltpu.VMEM((ROWS, columns), BF16),
            dma((7,)), dma((1,)), dma((1,)), dma((2,)), dma((2,)), dma((2, 4, 2)), dma((2, 4, 2)),
            dma((4, 7)), dma((4, 7)), dma((7,)), dma((7,)),
            dma((3,)), dma((3,)), dma((2, 4, 2)), dma((2, 4, 2)),
            dma((2,)), dma((2,)), dma((8,)), dma((8,)), dma((8,)), dma(()),
        ],
        compiler_params=pltpu.CompilerParams(
            collective_id=0, has_side_effects=True, vmem_limit_bytes=60 * 2**20
        ),
        cost_estimate=pl.CostEstimate(flops=13 * 10**9, bytes_accessed=4 * 10**6, transcendentals=4 * 10**6),
        name="attention",
    )(positions, kv_latent.T, kv_gain, q_nope, q_rope, kv_up, w_out.T)


def solution(mesh):
    return jax.shard_map(
        local,
        mesh=mesh,
        in_specs=(
            P("seq", "head"),
            P("seq", "head"),
            P("seq", None),
            P("seq"),
            P(),
            P(None, "head"),
            P("head", "seq"),
        ),
        out_specs=P("seq", "head"),
        check_vma=False,
    )
```

```python
import math

import jax
import jax.numpy as jnp
from jax import lax
from jax.experimental import pallas as pl
from jax.experimental.pallas import tpu as pltpu
from jax.sharding import PartitionSpec as P

KV_RANK = 512
ROPE = 64
NOPE = 128
VDIM = 128
ROWS = 128
HEADS = 8
WIDE = 640
PART = 256
HIDDEN = -1e30
MESH = pl.DeviceIdType.MESH
F32 = jnp.float32
BF16 = jnp.bfloat16


def dot_nt(a, b):
    return lax.dot_general(a, b, (((1,), (1,)), ((), ())), preferred_element_type=F32)


def kernel(
    pos_hbm, lat_hbm, gain_hbm, qn_hbm, qr_hbm, up_hbm, w_hbm, out_ref,
    pos_ref, lat_ref, gain_ref, keys, qn, qr, up, query, top, total, summed,
    held, w, part, half, strips, sums, reached, done, final,
    local_sem, x_send, x_recv, c_send, c_recv, z_send, z_recv, n_send, n_recv, d_send, d_recv,
    w_send, w_recv, a_send, a_recv, p_send, p_recv, s_send, s_recv, f_send, f_recv,
):
    s, head = lax.axis_index("seq"), lax.axis_index("head")
    z, xh, c, xl, y = s // 4, lax.rem(s // 2, 2), lax.rem(s, 2), head // 4, lax.rem(head, 4)

    def at(z, xh, c, xl, y):
        return (lax.rem(z + 8, 8) * 4 + xh * 2 + c, xl * 4 + lax.rem(y + 4, 4))

    def seat(plane, col):
        return (lax.rem(plane, 8) * 4 + xh * 2 + c, lax.rem(col, 8))

    def slab(k):
        return lax.rem(z + k + 8, 8)

    across, beside = at(z, 1 - xh, c, 1 - xl, y), at(z, xh, c, 1 - xl, y)
    partner, opposite = at(z, xh, 1 - c, xl, y), at(z, 1 - xh, c, xl, y)
    right, left = at(z + 1, xh, c, xl, y), at(z - 1, xh, c, xl, y)
    above, below = at(z, xh, c, xl, y + 1), at(z, xh, c, xl, y - 1)

    def remote(src, dst, send, recv, peer):
        return pltpu.make_async_remote_copy(
            src_ref=src, dst_ref=dst, send_sem=send, recv_sem=recv, device_id=peer, device_id_type=MESH
        )

    sent = []

    def push(src, dst, send, recv, peer):
        copy = remote(src, dst, send, recv, peer)
        copy.start()
        sent.append(copy)

    def landed(ref, send, recv):
        remote(ref, ref, send, recv, partner).wait_recv()

    def load(src, dst, i):
        copy = pltpu.make_async_copy(src, dst, local_sem.at[i])
        copy.start()
        return copy

    w_own = w.at[pl.ds(pl.multiple_of((xh * 2 + c) * 224, 32), 224)]
    first_loads = [load(lat_hbm, lat_ref, 0), load(gain_hbm, gain_ref, 1), load(pos_hbm, pos_ref, 2)]
    loads = [load(qn_hbm, qn, 3), load(up_hbm, up, 4), load(qr_hbm, qr, 5)]

    barrier = pltpu.get_barrier_semaphore()

    def greet(peer):
        pl.semaphore_signal(barrier, inc=1, device_id=peer, device_id_type=MESH)

    for peer in (across, partner, opposite, right, left, at(z + 1, 1 - xh, c, 1 - xl, y), at(z - 1, 1 - xh, c, 1 - xl, y)):
        greet(peer)
    for j in range(1, 8):
        greet(seat(z, head + j))
    for j in range(8):
        pl.when((head != z) | (head != j))(lambda: greet(seat(head, j)))

    for copy in first_loads:
        copy.wait()
    block_no = pos_ref[0] // ROWS
    lane = lax.broadcasted_iota(jnp.int32, (ROWS, 128), 1)
    coded = lat_ref[:KV_RANK, :].astype(F32).T
    latent = coded * lax.rsqrt(jnp.mean(coded * coded, axis=1, keepdims=True) + 1e-06)
    keys[z, xh, c, :, :KV_RANK] = (latent * gain_ref[...].reshape(1, KV_RANK)).astype(BF16)
    rope = lat_ref[KV_RANK:, :].astype(F32)
    tail = jnp.concatenate([rope, jnp.zeros((64, ROWS), F32)], axis=0).T
    keys[z, xh, c, :, KV_RANK:] = jnp.where(lane == 64 + block_no, 1.0, tail).astype(BF16)
    pl.semaphore_wait(barrier, jnp.where(head == z, 21, 22))

    colour = lax.rem(2 * (2 * xh + xl) + y, 4)

    def quarter(i, start=0, size=32):
        return pl.ds(pl.multiple_of(lax.rem(colour + i, 4) * 32 + start, 16), size)

    first, second = keys.at[z, xh, c, quarter(0)], keys.at[z, xh, c, quarter(2)]
    for way, step in ((0, 1), (1, -1)):
        push(first, first, z_send.at[way, 0, 0], z_recv.at[way, 0, 0], at(z + step, xh, c, xl, y))
        push(second, second, z_send.at[way, 0, 1], z_recv.at[way, 0, 1], at(z + step, 1 - xh, c, 1 - xl, y))
    push(keys.at[z, xh, c], keys.at[z, xh, c], x_send.at[0], x_recv.at[0], across)
    push(keys.at[z, xh, c], keys.at[z, xh, c], c_send.at[0], c_recv.at[0], partner)

    factor = math.log2(math.e) / math.sqrt(NOPE + ROPE)
    for copy in loads:
        copy.wait()
    ahead = jnp.where((lane >= 64) & (lane - 64 > block_no) & (lane < 96), HIDDEN, 0.0)

    def fold(h):
        rows = pl.ds(h * ROWS, ROWS)
        folded = dot_nt(qn[:, h * NOPE : (h + 1) * NOPE], up[:, h * 256 : h * 256 + NOPE])
        query[rows, :KV_RANK] = folded.astype(BF16)
        turned = qr[:, h * ROPE : (h + 1) * ROPE].astype(F32)
        turned = jnp.concatenate([turned, jnp.zeros((ROWS, 64), F32)], axis=1)
        query[rows, KV_RANK:] = (turned + ahead).astype(BF16)

    for h in range(4):
        fold(h)

    def w_piece(i):
        piece = pl.ds(pl.multiple_of((xh * 2 + c) * 224 + i * 32, 32), 32)
        remote(w_hbm.at[pl.ds(i * 32, 32)], w.at[piece], w_send.at[0], w_recv.at[0], opposite).start()

    def scores_of(k, i):
        return dot_nt(query[pl.ds(i * PART, PART), :], keys[slab(k)].reshape(512, WIDE))

    def absorb(k, i, scores):
        rows = pl.ds(i * PART, PART)
        if k == 0:
            own = xh * 256 + c * ROWS
            token = lax.rem(lax.broadcasted_iota(jnp.int32, (PART, 512), 0), ROWS)
            later = lax.broadcasted_iota(jnp.int32, (PART, 512), 1) - own
            scores = jnp.where((later > token) & (later < ROWS), HIDDEN, scores)
        most = jnp.max(scores, axis=1, keepdims=True)
        if k != 0:
            before = top[rows, :1]
            most = jnp.maximum(most, before)
            fade = jnp.exp2((before - most) * factor)
        expo = jnp.exp2((scores - most) * factor)
        mass = (expo[:, :128] + expo[:, 128:256]) + (expo[:, 256:384] + expo[:, 384:])
        values = keys[slab(k), :, :, :, :KV_RANK].reshape(512, KV_RANK)
        gained = jnp.dot(expo.astype(BF16), values, preferred_element_type=F32)
        if k == 0:
            summed[rows, :] = gained
            total[rows, :] = mass
        else:
            summed[rows, :] = summed[rows, :] * fade + gained
            total[rows, :] = total[rows, :] * fade + mass
        top[rows, :] = jnp.broadcast_to(most, (PART, 128))

    def attend(k, finish=None):
        count = HEADS * ROWS // PART
        following = scores_of(k, 0)
        for i in range(count):
            scores = following
            if i + 1 < count:
                following = scores_of(k, i + 1)
            absorb(k, i, scores)
            if finish is not None and (i + 1) % (count // 2) == 0:
                finish((i + 1) // (count // 2) - 1)

    slots = {-1: 0, 1: 1, -2: 2, 2: 3, -3: 4, 3: 5, 4: 6}

    def pass_on(k):
        i, block = slots[k], slab(k)
        mine = keys.at[block, :, c, quarter(0)]
        push(mine, mine, n_send.at[0, i], n_recv.at[0, i], above)
        push(mine, mine, n_send.at[1, i], n_recv.at[1, i], below)
        first, second = keys.at[block, :, c, quarter(0, 0, 16)], keys.at[block, :, c, quarter(0, 16, 16)]
        push(first, first, n_send.at[2, i], n_recv.at[2, i], beside)
        push(second, second, n_send.at[3, i], n_recv.at[3, i], across)

    def from_z(d):
        for t in (0, 1):
            kind = xh if t == 0 else 1 - xh
            for k, way, forward in ((-d, 0, right), (d, 1, left)):
                ref = keys.at[slab(k), kind, c, quarter(0)]
                if d < 4 or t == way:
                    landed(ref, z_send.at[way, d - 1, t], z_recv.at[way, d - 1, t])
                if d < 3 or (d == 3 and t == way):
                    push(ref, ref, z_send.at[way, d, t], z_recv.at[way, d, t], forward)
        for k in (-d, d) if d < 4 else (4,):
            pass_on(k)

    def from_plane(k):
        i, block = slots[k], slab(k)
        landed(keys.at[block, :, c, quarter(3)], n_send.at[0, i], n_recv.at[0, i])
        landed(keys.at[block, :, c, quarter(1)], n_send.at[1, i], n_recv.at[1, i])
        landed(keys.at[block, :, c, quarter(2, 0, 16)], n_send.at[2, i], n_recv.at[2, i])
        landed(keys.at[block, :, c, quarter(2, 16, 16)], n_send.at[3, i], n_recv.at[3, i])
        whole = keys.at[block, :, c]
        push(whole, whole, d_send.at[i], d_recv.at[i], partner)

    def ready(k):
        landed(keys.at[slab(k), :, 1 - c], d_send.at[slots[k]], d_recv.at[slots[k]])

    from_z(1)
    for h in range(4, 8):
        fold(h)
    from_z(2)
    theirs = keys.at[z, 1 - xh, c]
    landed(theirs, x_send.at[0], x_recv.at[0])
    push(theirs, theirs, c_send.at[1], c_recv.at[1], partner)
    w_copy = load(w_hbm, w_own, 6)
    w_piece(0)
    from_z(3)
    from_plane(-1)
    from_plane(1)
    landed(keys.at[z, xh, 1 - c], c_send.at[0], c_recv.at[0])
    landed(keys.at[z, 1 - xh, 1 - c], c_send.at[1], c_recv.at[1])
    attend(0)
    from_z(4)
    w_piece(1)
    w_piece(2)
    w_piece(3)
    from_plane(-2)
    ready(-1)
    attend(-1)
    from_plane(2)
    w_piece(4)
    w_piece(5)
    w_piece(6)
    push(w_hbm, w_own, w_send.at[1], w_recv.at[1], partner)
    ready(1)
    attend(1)
    from_plane(-3)
    ready(-2)
    attend(-2)
    from_plane(3)
    ready(2)
    attend(2)
    from_plane(4)
    ready(-3)
    attend(-3)
    ready(3)
    attend(3)
    ready(4)

    def finish(p):
        for h in range(4 * p, 4 * p + 4):
            rows = pl.ds(h * ROWS, ROWS)
            share = summed[rows, :] / jnp.sum(total[rows, :], axis=1, keepdims=True)
            value = jnp.dot(share.astype(BF16), up[:, h * 256 + NOPE : (h + 1) * 256], preferred_element_type=F32)
            held[z, p, :, (h - 4 * p) * VDIM : (h - 4 * p + 1) * VDIM] = value.astype(BF16)
        ref = held.at[z, p]
        push(ref, ref, a_send.at[0, 0, p], a_recv.at[0, 0, p], right)
        push(ref, ref, a_send.at[1, 0, p], a_recv.at[1, 0, p], left)

    attend(4, finish)

    earlier = sent[:-4]
    del sent[:-4]

    def flush(copies):
        for copy in copies:
            copy.wait_send()

    w_other = w.at[pl.ds(pl.multiple_of(((1 - xh) * 2 + c) * 224, 32), 224)]
    landed(w_other, w_send.at[0], w_recv.at[0])
    push(w_other, w_other, w_send.at[2], w_recv.at[2], partner)
    w_copy.wait()
    landed(w_other, w_send.at[1], w_recv.at[1])
    landed(w_other, w_send.at[2], w_recv.at[2])
    mine = pl.ds(pl.multiple_of(head * 16, 16), 16)

    lot = pl.ds(pl.multiple_of(y * 16, 16), 16)

    def lot_of(j):
        return pl.ds(pl.multiple_of(lax.rem(y + j, 4) * 16, 16), 16)

    def product(*offsets):
        sides = [jnp.concatenate([held[slab(k), p] for k in offsets], axis=0) for p in (0, 1)]
        both = dot_nt(sides[0], w[:, :512]) + dot_nt(sides[1], w[:, 512:])
        for n, k in enumerate(offsets):
            part[slab(k)] = both[n * ROWS : (n + 1) * ROWS].astype(BF16).reshape(2, 64, both.shape[1])
            spread(k)

    def spread(k):
        block = slab(k)
        if k == -3:
            push(part.at[block, 1 - xl], half, p_send.at[0], p_recv.at[0], beside)
        elif k == 3:
            for j in (1, 2, 3):
                remote(
                    part.at[block, :, lot_of(j)], strips.at[j - 1], p_send.at[1], p_recv.at[1], at(z, xh, c, xl, y + j)
                ).start()
        else:
            for j in range(1, 8):
                t = lax.rem(head + j, 8)
                rows = pl.ds(pl.multiple_of(lax.rem(t, 4) * 16, 16), 16)
                remote(
                    part.at[block, t // 4, rows], reached.at[block, j - 1], s_send.at[block], s_recv.at[block], seat(z, t)
                ).start()

    def relay(k):
        block = slab(k)
        if k == -3:
            landed(half, p_send.at[0], p_recv.at[0])
            half[...] = (part[block, xl].astype(F32) + half[...].astype(F32)).astype(BF16)
            for j in (1, 2, 3):
                remote(
                    half.at[lot_of(j)], reached.at[block, j - 1], s_send.at[block], s_recv.at[block],
                    at(z, xh, c, xl, y + j),
                ).start()
        else:
            landed(strips, p_send.at[1], p_recv.at[1])
            acc = part[block, :, lot].astype(F32)
            for j in range(3):
                acc = acc + strips[j].astype(F32)
            sums[...] = acc.astype(BF16)
            push(sums.at[1 - xl], reached.at[block, 0], s_send.at[block], s_recv.at[block], beside)

    def collect(k):
        block = slab(k)
        pieces = {-3: 3, 3: 1}.get(k, 7)
        landed(reached.at[block, pl.ds(0, pieces)], s_send.at[block], s_recv.at[block])
        if k == -3:
            acc = half[lot].astype(F32)
        elif k == 3:
            acc = sums[xl].astype(F32)
        else:
            acc = part[block, xl, lot].astype(F32)
        for j in range(pieces):
            acc = acc + reached[block, j].astype(F32)
        done[block] = acc.astype(BF16)
        if k == 0:

            @pl.when(head == z)
            def _():
                pltpu.make_async_copy(done.at[block], final.at[mine], f_recv).start()

            @pl.when(head != z)
            def _():
                remote(done.at[block], final.at[mine], f_send.at[0], f_recv, seat(block, z)).start()
        else:
            push(done.at[block], final.at[mine], f_send.at[k + 3], f_recv, seat(block, z))

    def from_ring(d, p):
        for k, way, forward in ((-d, 0, right), (d, 1, left)):
            ref = held.at[slab(k), p]
            landed(ref, a_send.at[way, d - 1, p], a_recv.at[way, d - 1, p])
            if d < 3 or p == way:
                push(ref, ref, a_send.at[way, d, p], a_recv.at[way, d, p], forward)

    product(0)
    flush(earlier)
    remote(w_other, w_other, w_send.at[0], w_recv.at[0], opposite).wait_send()
    from_ring(1, 0)
    from_ring(1, 1)
    product(-1, 1)
    from_ring(2, 0)
    collect(0)
    from_ring(2, 1)
    product(-2, 2)
    from_ring(3, 0)
    collect(-1)
    collect(1)
    from_ring(3, 1)
    product(-3, 3)
    collect(-2)
    collect(2)
    for way in (0, 1):
        landed(held.at[slab(4), way], a_send.at[way, 3, way], a_recv.at[way, 3, way])
    product(4)
    relay(-3)
    relay(3)
    collect(4)
    collect(-3)
    collect(3)
    for k in (0, -1, 1, -2, 2):
        remote(reached.at[slab(k)], reached.at[slab(k)], s_send.at[slab(k)], s_recv.at[slab(k)], right).wait_send()
    pieces = reached.at[slab(-3), pl.ds(0, 3)]
    remote(pieces, pieces, s_send.at[slab(-3)], s_recv.at[slab(-3)], right).wait_send()
    remote(strips, strips, p_send.at[1], p_recv.at[1], right).wait_send()
    for k in (4,):
        remote(reached.at[slab(k)], reached.at[slab(k)], s_send.at[slab(k)], s_recv.at[slab(k)], right).wait_send()
    flush(sent)

    @pl.when(head != z)
    def _():
        remote(done.at[0], done.at[0], f_send.at[0], f_recv, right).wait_send()

    landed(final, f_send.at[0], f_recv)
    out_ref[...] = final[...]


def local(q_nope, q_rope, kv_latent, positions, kv_gain, kv_up, w_out):
    dma = pltpu.SemaphoreType.DMA
    columns, depth = 4 * w_out.shape[1], w_out.shape[0]
    any_ = pl.BlockSpec(memory_space=pl.ANY)
    return pl.pallas_call(
        kernel,
        out_shape=pltpu.VMEM((ROWS, columns), BF16),
        in_specs=[any_] * 7,
        out_specs=pl.BlockSpec(memory_space=pltpu.VMEM),
        scratch_shapes=[
            pltpu.SMEM((ROWS,), jnp.int32),
            pltpu.VMEM((KV_RANK + ROPE, ROWS), BF16),
            pltpu.VMEM((KV_RANK,), F32),
            pltpu.VMEM((8, 2, 2, ROWS, WIDE), BF16),
            pltpu.VMEM((ROWS, HEADS * NOPE), BF16),
            pltpu.VMEM((ROWS, HEADS * ROPE), BF16),
            pltpu.VMEM((KV_RANK, HEADS * 256), BF16),
            pltpu.VMEM((HEADS * ROWS, WIDE), BF16),
            pltpu.VMEM((HEADS * ROWS, 128), F32),
            pltpu.VMEM((HEADS * ROWS, 128), F32),
            pltpu.VMEM((HEADS * ROWS, KV_RANK), F32),
            pltpu.VMEM((8, 2, ROWS, depth // 2), BF16),
            pltpu.VMEM((columns, depth), BF16),
            pltpu.VMEM((8, 2, 64, columns), BF16),
            pltpu.VMEM((64, columns), BF16),
            pltpu.VMEM((3, 2, 16, columns), BF16),
            pltpu.VMEM((2, 16, columns), BF16),
            pltpu.VMEM((8, 7, 16, columns), BF16),
            pltpu.VMEM((8, 16, columns), BF16),
            pltpu.VMEM((ROWS, columns), BF16),
            dma((7,)), dma((1,)), dma((1,)), dma((2,)), dma((2,)), dma((2, 4, 2)), dma((2, 4, 2)),
            dma((4, 7)), dma((4, 7)), dma((7,)), dma((7,)),
            dma((3,)), dma((3,)), dma((2, 4, 2)), dma((2, 4, 2)),
            dma((2,)), dma((2,)), dma((8,)), dma((8,)), dma((8,)), dma(()),
        ],
        compiler_params=pltpu.CompilerParams(
            collective_id=0, has_side_effects=True, vmem_limit_bytes=60 * 2**20
        ),
        cost_estimate=pl.CostEstimate(flops=13 * 10**9, bytes_accessed=4 * 10**6, transcendentals=4 * 10**6),
        name="attention",
    )(positions, kv_latent.T, kv_gain, q_nope, q_rope, kv_up, w_out.T)


def solution(mesh):
    return jax.shard_map(
        local,
        mesh=mesh,
        in_specs=(
            P("seq", "head"),
            P("seq", "head"),
            P("seq", None),
            P("seq"),
            P(),
            P(None, "head"),
            P("head", "seq"),
        ),
        out_specs=P("seq", "head"),
        check_vma=False,
    )
```
